512 devices in a mesh: az: 128 (over z, x, y_hi), ch: 4 (over y_lo, core).
Axes of the slice: x: 4, y: 8 (y_hi: 4, y_lo: 2; y = y_hi * 2 + y_lo), z: 8, core: 2. Of those that a mesh axis runs over, the one named last changes fastest.
Arguments:
- features: bfloat16 [256, 512, 256], P(None, 'az'), may hold values from -6 to 6
- conv1_weight: bfloat16 [256, 3, 3, 256], P('ch'), may hold values from -0.125 to 0.125
- conv1_bias: float32 [256], P('ch'), may hold values from -3 to 3
- conv2_weight: bfloat16 [256, 3, 3, 256], P('ch'), may hold values from -0.125 to 0.125
- conv2_bias: float32 [256], P('ch'), may hold values from -3 to 3
- request_cell: int32 [524288], P('az'), may hold values from 0 to 1023, as said below
- corner_slot: int32 [4, 65536], P(None, 'az'), may hold values from 0 to 4095, as said below
- corner_frac: float32 [2, 65536], P(None, 'az'), may hold values from 0 to 1
- expand_weight: bfloat16 [256, 512], P('ch'), may hold values from -0.375 to 0.375
- expand_bias: float32 [512], P('ch'), may hold values from -3 to 3
Outputs:
- occupancy: bfloat16 [512, 65536], P('ch', 'az')
The draws below stay inside these ranges and needn't reach their ends.
Inputs may be any that keep to these rules, and one draw needn't show every extreme that they name: `request_cell`: cell index a * 256 + r within the sector that the slot's block names; entries of slots that no corner_slot entry names are never read. `corner_slot`: within one tile the 2048 entries name distinct slots; at most 32 slots of one sector block are named, exactly 32 for some sector of every tile.
All inputs are finite; a program needn't handle non-finite values.
Results may differ from the reference program's by a relative error of at most 0.014.
Values may be sent and summed in bfloat16 or wider, within the bound.
A program may use at most 64 MiB of HBM per device.

```python
import jax
import jax.numpy as jnp
from jax import lax

C = 256
R = 256
CART_DEV = 512
A = 512
CELLS_DEV = 1024
CART = 65536
MEAN_REQ = 16
CAP = 32
HH = 512
N_AZ = 128
N_CH = 4


def tile_perm(subkey):
    return jax.random.permutation(subkey, 4 * CART_DEV)


def slot_table(key):
    base = jax.random.fold_in(key, 11)
    key_one, key_two, key_three, key_four = jax.random.split(base, 4)
    half = N_AZ // 2
    spread = jax.random.randint(key_one, (N_AZ, half), 0, MEAN_REQ + 1)
    chosen = jax.random.randint(key_two, (N_AZ,), 0, half)
    chosen = chosen.at[0].set(half - 1)
    sign_flip = jax.random.randint(key_three, (N_AZ, half), 0, 2) * 2 - 1
    sign_flip = sign_flip.at[0, half - 1].set(-1)
    marks = jnp.arange(half)[None, :] == chosen[:, None]
    spread = jnp.where(marks, MEAN_REQ, spread)
    counts = jnp.concatenate([MEAN_REQ + sign_flip * spread, MEAN_REQ - sign_flip * spread], axis=1)
    position = jnp.arange(CAP)
    used = (position[None, None, :] < counts[:, :, None]).reshape(N_AZ, N_AZ * CAP)
    order = jnp.argsort(1 - used.astype(jnp.int32), axis=1, stable=True)[:, :4 * CART_DEV]
    perms = jax.vmap(tile_perm)(jax.random.split(key_four, N_AZ))
    slots = jnp.take_along_axis(order, perms, axis=1)
    return slots.reshape(N_AZ, 4, CART_DEV).transpose(1, 0, 2).reshape(4, N_AZ * CART_DEV).astype(jnp.int32)


def draw_corner_slot(key, part):
    return slot_table(key)


def draw_request_cell(key, part):
    subkey = jax.random.fold_in(key, 23)
    cells = jax.random.randint(subkey, (N_AZ * N_AZ * CAP,), 0, CELLS_DEV)
    cells = cells.at[0].set(CELLS_DEV - 1)
    return cells.astype(jnp.int32)


def steps_of(stream_key, dims, cuts, least, top_value):
    def one(dim, shards_of):
        draws = jax.random.uniform(jax.random.fold_in(jax.random.fold_in(stream_key, 6), dim), (shards_of,), jnp.float32, least / len(cuts), top_value / len(cuts))
        return jnp.repeat(jnp.exp(draws), dims[dim] // shards_of).reshape((-1,) + (1,) * (len(dims) - dim - 1))

    level = one(*cuts[0])
    for cut in cuts[1:]:
        level = level * one(*cut)
    return level


def noise(stream_key, shape, scale, most, pieces=(), dtype=jnp.bfloat16):
    result = scale * jax.random.normal(stream_key, shape, jnp.float32)
    if pieces:
        result = result * steps_of(stream_key, shape, pieces, -0.22, 0.18)
    return jnp.clip(result, -most, most).astype(dtype)


def setup_inputs(seed: int = 0) -> dict:
    keys = jax.random.split(jax.random.key(seed), 11)
    features = noise(keys[0], (C, A, R), 1.0, 6.0, ((1, 128),))
    conv1_weight = noise(keys[1], (C, 3, 3, C), (9 * C) ** -0.5, 0.125, ((0, 4),))
    conv1_bias = noise(keys[2], (C,), 0.5, 3.0, ((0, 4),), jnp.float32)
    conv2_weight = noise(keys[3], (C, 3, 3, C), (9 * C) ** -0.5, 0.125, ((0, 4),))
    conv2_bias = noise(keys[4], (C,), 0.5, 3.0, ((0, 4),), jnp.float32)
    request_cell = draw_request_cell(jax.random.fold_in(keys[10], 71), 0)
    corner_slot = draw_corner_slot(jax.random.fold_in(keys[10], 71), 0)
    corner_frac = jnp.clip(1.0 * jax.random.uniform(keys[7], (2, CART), jnp.float32) ** steps_of(keys[7], (2, CART), ((1, 128),), -0.2, 0.2), 0.0, 1.0)
    expand_weight = noise(keys[8], (C, HH), C ** -0.5, 0.375, ((0, 4),))
    expand_bias = noise(keys[9], (HH,), 0.5, 3.0, ((0, 4),), jnp.float32)
    return dict(features=features, conv1_weight=conv1_weight, conv1_bias=conv1_bias, conv2_weight=conv2_weight, conv2_bias=conv2_bias, request_cell=request_cell, corner_slot=corner_slot, corner_frac=corner_frac, expand_weight=expand_weight, expand_bias=expand_bias)


def convolve(padded, weight, columns, ranges):
    inputs = padded.shape[0]
    ranged = jnp.pad(padded, ((0, 0), (0, 0), (1, 1)))
    running = jnp.zeros((weight.shape[0], columns * ranges), jnp.float32)
    for tap_az in range(3):
        for tap_rg in range(3):
            window = ranged[:, tap_az:tap_az + columns, tap_rg:tap_rg + ranges].reshape(inputs, columns * ranges)
            running = running + jnp.dot(weight[:, tap_az, tap_rg, :], window, preferred_element_type=jnp.float32)
    return running


def wrap_pad(field):
    return jnp.concatenate([field[:, -1:], field, field[:, :1]], axis=1)


def reference(features, conv1_weight, conv1_bias, conv2_weight, conv2_bias, request_cell, corner_slot, corner_frac, expand_weight, expand_bias):
    azimuths = features.shape[1]
    ranges = features.shape[2]
    hidden_one = jax.nn.relu(convolve(wrap_pad(features), conv1_weight, azimuths, ranges) + conv1_bias[:, None]).astype(jnp.bfloat16)
    hidden_one = hidden_one.reshape(-1, azimuths, ranges)
    hidden_two = jax.nn.relu(convolve(wrap_pad(hidden_one), conv2_weight, azimuths, ranges) + conv2_bias[:, None]).astype(jnp.bfloat16)
    table = request_cell.reshape(N_AZ, N_AZ * CAP)
    slots = corner_slot.reshape(4, N_AZ, CART_DEV)
    local_cells = jnp.take_along_axis(jnp.broadcast_to(table[None], (4,) + table.shape), slots, axis=2)
    global_cells = ((slots // CAP) * CELLS_DEV + local_cells).reshape(4, N_AZ * CART_DEV).astype(jnp.int32)
    frac_range = corner_frac[0][None, :]
    frac_azim = corner_frac[1][None, :]
    weights = [(1.0 - frac_range) * (1.0 - frac_azim), frac_range * (1.0 - frac_azim), (1.0 - frac_range) * frac_azim, frac_range * frac_azim]
    resampled = jnp.zeros((hidden_two.shape[0], N_AZ * CART_DEV), jnp.float32)
    for k in range(4):
        resampled = resampled + weights[k] * jnp.take(hidden_two, global_cells[k], axis=1).astype(jnp.float32)
    resampled = resampled.astype(jnp.bfloat16)
    group = expand_weight.shape[0] // N_CH
    summed = jnp.zeros((expand_weight.shape[1], N_AZ * CART_DEV), jnp.float32)
    for g in range(N_CH):
        partial_term = lax.dot_general(expand_weight[g * group:(g + 1) * group], resampled[g * group:(g + 1) * group], (((0,), (0,)), ((), ())), preferred_element_type=jnp.float32)
        rounded = lax.optimization_barrier(partial_term.astype(jnp.bfloat16))
        summed = summed + rounded.astype(jnp.float32)
    return (summed + expand_bias[:, None]).astype(jnp.bfloat16)
```

```python
import functools

import jax
import jax.numpy as jnp
from jax import lax
from jax.experimental import pallas as pl
from jax.experimental.pallas import tpu as pltpu
from jax.sharding import PartitionSpec as P

MESH = pl.DeviceIdType.MESH
BF = jnp.bfloat16
F32 = jnp.float32
HALF = 16


def group_of(n):
    return 8 if n % 64 == 0 else 2


def combine(acc, rows, ranges):
    lane = lax.broadcasted_iota(jnp.int32, (rows, ranges), 1)
    low = jnp.where(lane == 0, 0.0, pltpu.roll(acc[:rows], 1, 1))
    high = jnp.where(lane == ranges - 1, 0.0, pltpu.roll(acc[2 * rows :], ranges - 1, 1))
    return low + acc[rows : 2 * rows] + high


def column_of(row):
    k = row.shape[1]
    a = lax.broadcasted_iota(jnp.int32, (k, k), 0)
    b = lax.broadcasted_iota(jnp.int32, (k, k), 1)
    return jnp.sum(jnp.where(a == b, jnp.broadcast_to(row, (k, k)), 0.0), axis=1, keepdims=True)


def kernel(
    n,
    feat,
    w1,
    b1,
    w2,
    b2,
    req,
    slot,
    frac,
    wexp,
    bexp,
    out,
    h1,
    e1s,
    e1r,
    e2s,
    e2r,
    acc_edge,
    oha,
    ohb,
    sa,
    sb,
    keyt,
    wt,
    reqt,
    pbuf,
    arr,
    h2t,
    rq,
    wr,
    wx,
    rbuf,
    e1_send,
    e1_recv,
    e2_send,
    e2_recv,
    rq_send,
    rq_recv,
    w_send,
    w_recv,
    g_send,
    g_recv,
    r_send,
    r_recv,
    a_send,
    a_recv,
):
    az = lax.axis_index("az")
    ch = lax.axis_index("ch")
    chans = feat.shape[0] // 4
    ranges = feat.shape[1]
    outs = w1.shape[0] // 3
    cart = slot.shape[1]
    groups = group_of(n)
    members = n // groups
    rows = members * HALF
    hh = out.shape[0]
    right = lax.rem(az + 1, n)
    left = lax.rem(az + n - 1, n)

    barrier = pltpu.get_barrier_semaphore()

    def greet(d, _):
        pl.semaphore_signal(
            barrier, inc=1, device_id=(lax.rem(az + d, n), ch), device_id_type=MESH
        )
        return 0

    lax.fori_loop(1, n, greet, 0)
    for d in range(1, 4):
        pl.semaphore_signal(
            barrier, inc=1, device_id=(az, lax.rem(ch + d, 4)), device_id_type=MESH
        )

    def part(w, x, col):
        lo, hi = max(col - 1, 0), min(col + 1, 3)
        first = lo - (col - 1)
        return jnp.dot(
            w[:, first * chans : (first + hi - lo + 1) * chans],
            x[lo * chans : (hi + 1) * chans, :],
            preferred_element_type=F32,
        )

    e1s[0] = combine(part(w1, feat, 4), outs, ranges).astype(BF)
    e1s[1] = combine(part(w1, feat, -1), outs, ranges).astype(BF)

    pl.semaphore_wait(barrier, n + 2)

    def edge(src, dst, send, recv):
        copies = []
        for k, to in ((0, right), (1, left)):
            copies.append(
                pltpu.make_async_remote_copy(
                    src_ref=src.at[k],
                    dst_ref=dst.at[k],
                    send_sem=send.at[k],
                    recv_sem=recv.at[k],
                    device_id=(to, ch),
                    device_id_type=MESH,
                )
            )
        return copies

    e1 = edge(e1s, e1r, e1_send, e1_recv)
    for c in e1:
        c.start()

    def ask(d, _):
        to = lax.rem(az + d, n)
        pltpu.make_async_remote_copy(
            src_ref=req.at[to],
            dst_ref=rq.at[az],
            send_sem=rq_send,
            recv_sem=rq_recv,
            device_id=(to, ch),
            device_id_type=MESH,
        ).start()
        return 0

    lax.fori_loop(1, n, ask, 0)
    wcopies = []
    for d in range(1, 4):
        to = lax.rem(ch + d, 4)
        c = pltpu.make_async_remote_copy(
            src_ref=wexp.at[to],
            dst_ref=wr.at[ch],
            send_sem=w_send.at[d - 1],
            recv_sem=w_recv.at[d - 1],
            device_id=(az, to),
            device_id_type=MESH,
        )
        c.start()
        wcopies.append(c)
    wr[ch] = wexp[ch]
    rq[az] = req[az]

    bias1 = column_of(b1[...])
    bias2 = column_of(b2[...])

    def finish(total, bias):
        return jnp.maximum(total + bias, 0.0).astype(BF)

    def mine(col):
        return pl.ds(pl.multiple_of(col * chans + ch * outs, outs), outs)

    def spread(col):
        copies = []
        for d in range(1, 4):
            c = pltpu.make_async_remote_copy(
                src_ref=h1.at[mine(col)],
                dst_ref=h1.at[mine(col)],
                send_sem=g_send.at[col, d - 1],
                recv_sem=g_recv.at[col, d - 1],
                device_id=(az, lax.rem(ch + d, 4)),
                device_id_type=MESH,
            )
            c.start()
            copies.append(c)
        return copies

    gathers = {}
    for col in (1, 2):
        h1[mine(col), :] = finish(combine(part(w1, feat, col), outs, ranges), bias1)
        gathers[col] = spread(col)
    for k, col in ((0, 0), (1, 3)):
        acc_edge[k] = combine(part(w1, feat, col), outs, ranges) + bias1
    for k, col in ((0, 0), (1, 3)):
        e1[k].wait_recv()
        h1[mine(col), :] = jnp.maximum(acc_edge[k] + e1r[k].astype(F32), 0.0).astype(BF)
        gathers[col] = spread(col)

    q = slot[...]
    m = lax.shift_left(lax.shift_right_logical(q, 5), 4) + jnp.bitwise_and(q, 15)
    upper = jnp.bitwise_and(q, 16) != 0
    keys = jnp.concatenate(
        [jnp.where(upper, -1, m), jnp.where(upper, m, -1)]
        + [jnp.zeros((120, cart), jnp.int32)],
        axis=0,
    )
    keyt[...] = keys.T
    u, v = frac[0:1, :], frac[1:2, :]
    weights = jnp.concatenate(
        [(1.0 - u) * (1.0 - v), u * (1.0 - v), (1.0 - u) * v, u * v]
        + [jnp.zeros((124, cart), F32)],
        axis=0,
    )
    wt[...] = weights.T

    def s_rows(b, _):
        at = pl.ds(pl.multiple_of(b * 16, 16), 16)
        spot = lax.broadcasted_iota(jnp.int32, (16, n * HALF), 1)
        for base, ref in ((0, sa), (4, sb)):
            total = jnp.zeros((16, n * HALF), F32)
            for k in range(4):
                key = keyt[at, base + k : base + k + 1]
                total = jnp.where(spot == key, wt[at, k : k + 1], total)
            ref[at, :] = total.astype(BF)
        return 0

    lax.fori_loop(0, cart // 16, s_rows, 0)

    for d in range(3):
        wcopies[d].wait_recv()
    for g in range(4):
        block = wr[g].astype(F32)
        zero = jnp.zeros((128 - outs, hh), F32)
        wx[0, :, g * 128 : (g + 1) * 128] = jnp.concatenate([block, zero], axis=0).T.astype(BF)
        wx[1, :, g * 128 : (g + 1) * 128] = jnp.concatenate([zero, block], axis=0).T.astype(BF)
    bias3 = column_of(bexp[...])

    for col in (3, 0):
        for c in gathers[col]:
            c.wait_recv()
    e2s[0] = combine(part(w2, h1, 4), outs, ranges).astype(BF)
    e2s[1] = combine(part(w2, h1, -1), outs, ranges).astype(BF)
    e2 = edge(e2s, e2r, e2_send, e2_recv)
    for c in e2:
        c.start()
    for col in (1, 2):
        for c in gathers[col]:
            c.wait_recv()

    def place(col, value):
        zero = jnp.zeros((128 - outs, ranges), F32)
        at = slice(col * ranges, (col + 1) * ranges)
        h2t[0, at, :] = jnp.concatenate([value, zero], axis=0).T.astype(BF)
        h2t[1, at, :] = jnp.concatenate([zero, value], axis=0).T.astype(BF)

    for col in (1, 2):
        place(col, jnp.maximum(combine(part(w2, h1, col), outs, ranges) + bias2, 0.0))
    for k, col in ((0, 0), (1, 3)):
        acc_edge[k] = combine(part(w2, h1, col), outs, ranges) + bias2

    pltpu.make_async_remote_copy(
        src_ref=req.at[pl.ds(0, n - 1)],
        dst_ref=rq.at[pl.ds(0, n - 1)],
        send_sem=rq_send,
        recv_sem=rq_recv,
        device_id=(right, ch),
        device_id_type=MESH,
    ).wait_recv()
    reqt[...] = rq[:, 0, :].T

    def one_hot(t, _):
        turned = pltpu.roll(reqt[...], lax.rem(n - t, n), 1)
        spot = lax.broadcasted_iota(jnp.int32, (HALF, 4 * ranges), 1)
        at = pl.ds(pl.multiple_of(t * HALF, HALF), HALF)
        oha[at, :] = jnp.where(spot == turned[:HALF, 0:1], 1.0, 0.0).astype(BF)
        ohb[at, :] = jnp.where(spot == turned[HALF : 2 * HALF, 0:1], 1.0, 0.0).astype(BF)
        return 0

    lax.fori_loop(0, n, one_hot, 0)

    for k, col in ((0, 0), (1, 3)):
        e2[k].wait_recv()
        place(col, jnp.maximum(acc_edge[k] + e2r[k].astype(F32), 0.0))

    plane = az // members
    inner = lax.rem(az, members)
    for dz in range(groups):
        to_plane = lax.rem(plane + dz, groups)
        at = pl.ds(pl.multiple_of(to_plane * rows, rows), rows)
        picked = jnp.dot(oha[at, :], h2t[0], preferred_element_type=F32)
        picked += jnp.dot(ohb[at, :], h2t[1], preferred_element_type=F32)
        pbuf[dz] = picked.astype(BF)

        def ship(i, _):
            spot = lax.rem(inner + i, members)
            pltpu.make_async_remote_copy(
                src_ref=pbuf.at[dz, pl.ds(pl.multiple_of(spot * HALF, HALF), HALF)],
                dst_ref=arr.at[dz, pl.ds(pl.multiple_of(inner * HALF, HALF), HALF)],
                send_sem=a_send.at[dz],
                recv_sem=a_recv.at[dz],
                device_id=(to_plane * members + spot, ch),
                device_id_type=MESH,
            ).start()
            return 0

        lax.fori_loop(1 if dz == 0 else 0, members, ship, 0)
        if dz == 0:
            own = pl.ds(pl.multiple_of(inner * HALF, HALF), HALF)
            arr[0, own, :] = pbuf[0, own, :]

    def whole(dz):
        size = rows - HALF if dz == 0 else rows
        return pltpu.make_async_remote_copy(
            src_ref=pbuf.at[dz, pl.ds(0, size)],
            dst_ref=arr.at[dz, pl.ds(0, size)],
            send_sem=a_send.at[dz],
            recv_sem=a_recv.at[dz],
            device_id=(right, ch),
            device_id_type=MESH,
        )

    total_a = jnp.zeros((cart, 128), F32)
    total_b = jnp.zeros((cart, 128), F32)
    for dz in range(groups):
        whole(dz).wait_recv()
        from_plane = lax.rem(plane + groups - dz, groups)
        at = pl.ds(pl.multiple_of(from_plane * rows, rows), rows)
        total_a += jnp.dot(sa[:, at], arr[dz], preferred_element_type=F32)
        total_b += jnp.dot(sb[:, at], arr[dz], preferred_element_type=F32)

    half = cart // 2
    lane = lax.broadcasted_iota(jnp.int32, (half, 128), 1)
    first = total_a[:half] + pltpu.roll(total_b[:half], 64, 1)
    second = pltpu.roll(total_a[half:], 64, 1) + total_b[half:]
    rbuf[ch] = jnp.where(lane < 64, first, second).astype(BF)
    rcopies = []
    for d in range(1, 4):
        c = pltpu.make_async_remote_copy(
            src_ref=rbuf.at[ch],
            dst_ref=rbuf.at[ch],
            send_sem=r_send.at[d - 1],
            recv_sem=r_recv.at[d - 1],
            device_id=(az, lax.rem(ch + d, 4)),
            device_id_type=MESH,
        )
        c.start()
        rcopies.append(c)
    for c in rcopies:
        c.wait_recv()
    for p in range(2):
        sum_p = jnp.zeros((hh, half), F32)
        for g in range(4):
            sum_p += lax.dot_general(
                wx[p, :, g * 128 : (g + 1) * 128],
                rbuf[g],
                (((1,), (1,)), ((), ())),
                preferred_element_type=F32,
            )
        out[:, p * half : (p + 1) * half] = (sum_p + bias3).astype(BF)

    for c in e1 + e2 + wcopies + rcopies + [c for col in range(4) for c in gathers[col]]:
        c.wait_send()
    pltpu.make_async_remote_copy(
        src_ref=req.at[pl.ds(0, n - 1)],
        dst_ref=rq.at[pl.ds(0, n - 1)],
        send_sem=rq_send,
        recv_sem=rq_recv,
        device_id=(right, ch),
        device_id_type=MESH,
    ).wait_send()
    for dz in range(groups):
        whole(dz).wait_send()


def local(
    features,
    conv1_weight,
    conv1_bias,
    conv2_weight,
    conv2_bias,
    request_cell,
    corner_slot,
    corner_frac,
    expand_weight,
    expand_bias,
):
    n = lax.axis_size("az")
    chans, columns, ranges = features.shape
    outs = conv1_weight.shape[0]
    cart = corner_slot.shape[1]
    hh = expand_bias.shape[0]
    groups = group_of(n)
    rows = n // groups * HALF

    feat = features.transpose(1, 0, 2).reshape(columns * chans, ranges)
    w1 = conv1_weight.transpose(2, 0, 1, 3).reshape(3 * outs, 3 * chans)
    w2 = conv2_weight.transpose(2, 0, 1, 3).reshape(3 * outs, 3 * chans)
    wexp = expand_weight.reshape(outs, 4, hh).transpose(1, 0, 2)
    args = (
        feat,
        w1,
        conv1_bias.reshape(1, outs),
        w2,
        conv2_bias.reshape(1, outs),
        request_cell.reshape(n, 1, 2 * HALF),
        corner_slot,
        corner_frac,
        wexp,
        expand_bias.reshape(1, hh),
    )
    dma = pltpu.SemaphoreType.DMA
    return pl.pallas_call(
        functools.partial(kernel, n),
        out_shape=jax.ShapeDtypeStruct((hh, cart), BF),
        in_specs=[pl.BlockSpec(memory_space=pltpu.VMEM)] * len(args),
        out_specs=pl.BlockSpec(memory_space=pltpu.VMEM),
        scratch_shapes=[
            pltpu.VMEM((4 * chans, ranges), BF),
            pltpu.VMEM((2, outs, ranges), BF),
            pltpu.VMEM((2, outs, ranges), BF),
            pltpu.VMEM((2, outs, ranges), BF),
            pltpu.VMEM((2, outs, ranges), BF),
            pltpu.VMEM((2, outs, ranges), F32),
            pltpu.VMEM((n * HALF, 4 * ranges), BF),
            pltpu.VMEM((n * HALF, 4 * ranges), BF),
            pltpu.VMEM((cart, n * HALF), BF),
            pltpu.VMEM((cart, n * HALF), BF),
            pltpu.VMEM((cart, 128), jnp.int32),
            pltpu.VMEM((cart, 128), F32),
            pltpu.VMEM((2 * HALF, n), jnp.int32),
            pltpu.VMEM((groups, rows, 128), BF),
            pltpu.VMEM((groups, rows, 128), BF),
            pltpu.VMEM((2, 4 * ranges, 128), BF),
            pltpu.VMEM((n, 1, 2 * HALF), jnp.int32),
            pltpu.VMEM((4, outs, hh), BF),
            pltpu.VMEM((2, hh, 512), BF),
            pltpu.VMEM((4, cart // 2, 128), BF),
            dma((2,)),
            dma((2,)),
            dma((2,)),
            dma((2,)),
            dma,
            dma,
            dma((3,)),
            dma((3,)),
            dma((4, 3)),
            dma((4, 3)),
            dma((3,)),
            dma((3,)),
            dma((groups,)),
            dma((groups,)),
        ],
        compiler_params=pltpu.CompilerParams(
            collective_id=0, has_side_effects=True, vmem_limit_bytes=40 * 1024 * 1024
        ),
        cost_estimate=pl.CostEstimate(
            flops=4 * 10**9, bytes_accessed=2 * 10**6, transcendentals=0
        ),
    )(*args)


def solution(mesh):
    return jax.shard_map(
        local,
        mesh=mesh,
        in_specs=(
            P(None, "az", None),
            P("ch", None, None, None),
            P("ch"),
            P("ch", None, None, None),
            P("ch"),
            P("az"),
            P(None, "az"),
            P(None, "az"),
            P("ch", None),
            P("ch"),
        ),
        out_specs=P("ch", "az"),
        check_vma=False,
    )
```

```python
import functools

import jax
import jax.numpy as jnp
from jax import lax
from jax.experimental import pallas as pl
from jax.experimental.pallas import tpu as pltpu
from jax.sharding import PartitionSpec as P

MESH = pl.DeviceIdType.MESH
BF = jnp.bfloat16
F32 = jnp.float32
HALF = 16


def torus(n):
    return (8, 4, 4) if n == 128 else (2, 1, n // 2)


def combine(acc, rows, ranges):
    lane = lax.broadcasted_iota(jnp.int32, (rows, ranges), 1)
    low = jnp.where(lane == 0, 0.0, pltpu.roll(acc[:rows], 1, 1))
    high = jnp.where(lane == ranges - 1, 0.0, pltpu.roll(acc[2 * rows :], ranges - 1, 1))
    return low + acc[rows : 2 * rows] + high


def column_of(row):
    k = row.shape[1]
    a = lax.broadcasted_iota(jnp.int32, (k, k), 0)
    b = lax.broadcasted_iota(jnp.int32, (k, k), 1)
    return jnp.sum(jnp.where(a == b, jnp.broadcast_to(row, (k, k)), 0.0), axis=1, keepdims=True)


def kernel(
    n,
    feat,
    w1_in,
    b1_in,
    w2_in,
    b2_in,
    req_in,
    slot_in,
    frac_in,
    wexp,
    b3_in,
    out,
    fv,
    x1,
    w1,
    b1,
    w2,
    b2,
    req,
    slot,
    frac,
    b3,
    h1,
    e1s,
    e1r,
    e2s,
    e2r,
    acc_edge,
    oha,
    ohb,
    sa,
    sb,
    keyt,
    wt,
    reqt,
    reqg,
    pbuf,
    arr,
    h2t,
    rq,
    wr,
    wx,
    rbuf,
    in_sem,
    e1_send,
    e1_recv,
    e2_send,
    e2_recv,
    rq_send,
    rq_recv,
    rg_send,
    rg_recv,
    w_send,
    w_recv,
    g_send,
    g_recv,
    r_send,
    r_recv,
    a_send,
    a_recv,
):
    az = lax.axis_index("az")
    ch = lax.axis_index("ch")
    nz, nx, ny = torus(n)
    members = nx * ny
    groups = nz
    chans = x1.shape[0] // 4
    ranges = x1.shape[1]
    outs = w1.shape[0] // 9
    cart = slot.shape[1]
    rows = members * HALF
    hh = out.shape[0]
    share = n // 4
    right = lax.rem(az + 1, n)
    left = lax.rem(az + n - 1, n)
    my_z = az // members
    my_x = lax.rem(az, members) // ny
    my_y = lax.rem(az, ny)

    barrier = pltpu.get_barrier_semaphore()

    def greet(d, _):
        to = az + d
        pl.semaphore_signal(
            barrier,
            inc=1,
            device_id=(jnp.where(to >= n, to - n, to), ch),
            device_id_type=MESH,
        )
        return 0

    lax.fori_loop(1, n, greet, 0, unroll=True)
    for d in range(1, 4):
        pl.semaphore_signal(
            barrier, inc=1, device_id=(az, lax.rem(ch + d, 4)), device_id_type=MESH
        )

    fetches = []
    pairs = (
        (feat, fv),
        (w1_in, w1),
        (req_in, req),
        (b1_in, b1),
        (w2_in, w2),
        (b2_in, b2),
        (slot_in, slot),
        (frac_in, frac),
        (b3_in, b3),
    )
    for k, (src, dst) in enumerate(pairs):
        c = pltpu.make_async_copy(src, dst, in_sem.at[k])
        c.start()
        fetches.append(c)

    def at_column(col):
        return slice(col * chans, (col + 1) * chans)

    def part(w, x, col):
        total = None
        for tap in range(3):
            src = col + tap - 1
            if 0 <= src <= 3:
                term = jnp.dot(
                    w[tap * 3 * outs : (tap + 1) * 3 * outs, :],
                    x[at_column(src), :],
                    preferred_element_type=F32,
                )
                total = term if total is None else total + term
        return combine(total, outs, ranges)

    fetches[0].wait()
    for col in range(4):
        x1[at_column(col), :] = fv[:, col, :]
    fetches[1].wait()
    e1s[0] = part(w1, x1, 4).astype(BF)
    e1s[1] = part(w1, x1, -1).astype(BF)
    fetches[2].wait()

    pl.semaphore_wait(barrier, n + 2)

    def edge(src, dst, send, recv):
        copies = []
        for k, to in ((0, right), (1, left)):
            copies.append(
                pltpu.make_async_remote_copy(
                    src_ref=src.at[k],
                    dst_ref=dst.at[k],
                    send_sem=send.at[k],
                    recv_sem=recv.at[k],
                    device_id=(to, ch),
                    device_id_type=MESH,
                )
            )
        return copies

    e1 = edge(e1s, e1r, e1_send, e1_recv)
    for c in e1:
        c.start()

    def shifted(g, i, sign):
        dz = lax.rem(g + i, nz)
        dx = i // ny
        dy = lax.rem(i, ny)
        if sign > 0:
            z, x, y = my_z + dz, my_x + dx, my_y + dy
        else:
            z, x, y = my_z + nz - dz, my_x + nx - dx, my_y + ny - dy
        return lax.rem(z, nz) * members + lax.rem(x, nx) * ny + lax.rem(y, ny)

    def ask(k, _):
        p = ch * share + k
        to = shifted(p // members, lax.rem(p, members), -1)
        pltpu.make_async_remote_copy(
            src_ref=req.at[to // 4],
            dst_ref=rq.at[p],
            send_sem=rq_send,
            recv_sem=rq_recv,
            device_id=(to, ch),
            device_id_type=MESH,
        ).start()
        return 0

    @pl.when(ch == 0)
    def _():
        pltpu.make_async_copy(req.at[az // 4], rq.at[0], rq_recv).start()

    lax.fori_loop(jnp.where(ch == 0, 1, 0), share, ask, 0)

    wcopies = []
    for d in range(1, 4):
        to = lax.rem(ch + d, 4)
        c = pltpu.make_async_remote_copy(
            src_ref=wexp.at[:, pl.ds(pl.multiple_of(to * hh, hh), hh)],
            dst_ref=wr.at[ch],
            send_sem=w_send.at[d - 1],
            recv_sem=w_recv.at[d - 1],
            device_id=(az, to),
            device_id_type=MESH,
        )
        c.start()
        wcopies.append(c)
    own_w = pltpu.make_async_copy(
        wexp.at[:, pl.ds(pl.multiple_of(ch * hh, hh), hh)], wr.at[ch], in_sem.at[len(pairs)]
    )
    own_w.start()

    fetches[3].wait()
    bias1 = column_of(b1[...])

    def mine(col):
        return pl.ds(pl.multiple_of(col * chans + ch * outs, outs), outs)

    def spread(col):
        copies = []
        for d in range(1, 4):
            c = pltpu.make_async_remote_copy(
                src_ref=h1.at[mine(col)],
                dst_ref=h1.at[mine(col)],
                send_sem=g_send.at[col, d - 1],
                recv_sem=g_recv.at[col, d - 1],
                device_id=(az, lax.rem(ch + d, 4)),
                device_id_type=MESH,
            )
            c.start()
            copies.append(c)
        return copies

    gathers = {}
    for col in (1, 2):
        h1[mine(col), :] = jnp.maximum(part(w1, x1, col) + bias1, 0.0).astype(BF)
        gathers[col] = spread(col)
    for k, col in ((0, 0), (1, 3)):
        acc_edge[k] = part(w1, x1, col) + bias1

    def asked(ref, at, count, send, recv):
        return pltpu.make_async_remote_copy(
            src_ref=ref.at[pl.ds(at, count)],
            dst_ref=ref.at[pl.ds(at, count)],
            send_sem=send,
            recv_sem=recv,
            device_id=(right, ch),
            device_id_type=MESH,
        )

    asked(rq, 0, share, rq_send, rq_recv).wait_recv()
    passed = []
    for d in range(1, 4):
        at = pl.ds(pl.multiple_of(ch * share, share), share)
        c = pltpu.make_async_remote_copy(
            src_ref=rq.at[at],
            dst_ref=rq.at[at],
            send_sem=rg_send.at[d - 1],
            recv_sem=rg_recv.at[d - 1],
            device_id=(az, lax.rem(ch + d, 4)),
            device_id_type=MESH,
        )
        passed.append(c)

    for k, col in ((0, 0), (1, 3)):
        e1[k].wait_recv()
        h1[mine(col), :] = jnp.maximum(acc_edge[k] + e1r[k].astype(F32), 0.0).astype(BF)
        gathers[col] = spread(col)
    for c in passed:
        c.start()

    for c in fetches[4:]:
        c.wait()
    q = slot[...]
    sector = lax.shift_right_logical(q, 5)
    low = jnp.bitwise_and(q, HALF - 1)
    upper = jnp.bitwise_and(q, HALF) != 0
    dx = jnp.bitwise_and(my_x - jnp.bitwise_and(sector // ny, nx - 1), nx - 1)
    dy = jnp.bitwise_and(my_y - jnp.bitwise_and(sector, ny - 1), ny - 1)
    place_i = dx * ny + dy
    place_g = jnp.bitwise_and(my_z - sector // members - place_i, nz - 1)
    m = (place_g * members + place_i) * HALF + low
    keys = jnp.concatenate(
        [jnp.where(upper, -1, m), jnp.where(upper, m, -1)]
        + [jnp.zeros((120, cart), jnp.int32)],
        axis=0,
    )
    keyt[...] = keys.T
    u, v = frac[0:1, :], frac[1:2, :]
    weights = jnp.concatenate(
        [(1.0 - u) * (1.0 - v), u * (1.0 - v), (1.0 - u) * v, u * v]
        + [jnp.zeros((124, cart), F32)],
        axis=0,
    )
    wt[...] = weights.T
    width = min(128, n * HALF)

    def s_rows(b, _):
        at = pl.ds(pl.multiple_of(b * 16, 16), 16)
        spot = lax.broadcasted_iota(jnp.int32, (16, width), 1).astype(jnp.int16)
        parts = [jnp.broadcast_to(wt[at, k : k + 1], (16, width)).astype(BF) for k in range(4)]
        for base, ref in ((0, sa), (4, sb)):
            found = [
                jnp.broadcast_to(keyt[at, base + k : base + k + 1], (16, width)).astype(jnp.int16)
                for k in range(4)
            ]
            for j in range(n * HALF // width):
                here = spot + jnp.int16(j * width)
                total = jnp.zeros((16, width), BF)
                for k in range(4):
                    total = jnp.where(here == found[k], parts[k], total)
                ref[at, j * width : (j + 1) * width] = total
        return 0

    lax.fori_loop(0, cart // 16, s_rows, 0, unroll=2 if cart >= 32 else 1)

    for col in (3, 0):
        for c in gathers[col]:
            c.wait_recv()
    e2s[0] = part(w2, h1, 4).astype(BF)
    e2s[1] = part(w2, h1, -1).astype(BF)
    e2 = edge(e2s, e2r, e2_send, e2_recv)
    for c in e2:
        c.start()
    for col in (1, 2):
        for c in gathers[col]:
            c.wait_recv()

    def place(col, value):
        zero = jnp.zeros((128 - outs, ranges), F32)
        at = slice(col * ranges, (col + 1) * ranges)
        h2t[0, at, :] = jnp.concatenate([value, zero], axis=0).T.astype(BF)
        h2t[1, at, :] = jnp.concatenate([zero, value], axis=0).T.astype(BF)

    bias2 = column_of(b2[...])
    for col in (1, 2):
        place(col, jnp.maximum(part(w2, h1, col) + bias2, 0.0))
    for k, col in ((0, 0), (1, 3)):
        acc_edge[k] = part(w2, h1, col) + bias2

    for c in passed:
        c.wait_recv()
    reqt[...] = rq[:, 0, :].T
    wanted = reqt[pl.ds(pl.multiple_of(lax.rem(az, 4) * 2 * HALF, 2 * HALF), 2 * HALF), :]
    for g in range(groups):
        reqg[g] = wanted[:, g * members : (g + 1) * members]

    def one_hot(g, _):
        some = reqg[g]
        spot = lax.broadcasted_iota(jnp.int32, (HALF, 4 * ranges), 1)
        for i in range(members):
            at = pl.ds(pl.multiple_of(g * rows + i * HALF, HALF), HALF)
            oha[at, :] = jnp.where(spot == some[:HALF, i : i + 1], 1.0, 0.0).astype(BF)
            ohb[at, :] = jnp.where(spot == some[HALF:, i : i + 1], 1.0, 0.0).astype(BF)
        return 0

    lax.fori_loop(0, groups, one_hot, 0)

    own_w.wait()
    for d in range(3):
        wcopies[d].wait_recv()
    for g in range(4):
        block = wr[g].astype(F32)
        zero = jnp.zeros((128 - outs, hh), F32)
        wx[0, :, g * 128 : (g + 1) * 128] = jnp.concatenate([block, zero], axis=0).T.astype(BF)
        wx[1, :, g * 128 : (g + 1) * 128] = jnp.concatenate([zero, block], axis=0).T.astype(BF)
    bias3 = column_of(b3[...])

    for k, col in ((0, 0), (1, 3)):
        e2[k].wait_recv()
        place(col, jnp.maximum(acc_edge[k] + e2r[k].astype(F32), 0.0))

    for g in range(groups):
        at = slice(g * rows, (g + 1) * rows)
        picked = jnp.dot(oha[at, :], h2t[0], preferred_element_type=F32)
        picked += jnp.dot(ohb[at, :], h2t[1], preferred_element_type=F32)
        pbuf[g] = picked.astype(BF)

        def ship(i, _):
            block = pl.ds(pl.multiple_of(i * HALF, HALF), HALF)
            pltpu.make_async_remote_copy(
                src_ref=pbuf.at[g, block],
                dst_ref=arr.at[g, block],
                send_sem=a_send.at[g],
                recv_sem=a_recv.at[g],
                device_id=(shifted(g, i, 1), ch),
                device_id_type=MESH,
            ).start()
            return 0

        lax.fori_loop(1 if g == 0 else 0, members, ship, 0)
        if g == 0:
            arr[0, :HALF, :] = pbuf[0, :HALF, :]

    def whole(g):
        size = rows - HALF if g == 0 else rows
        return pltpu.make_async_remote_copy(
            src_ref=pbuf.at[g, pl.ds(0, size)],
            dst_ref=arr.at[g, pl.ds(0, size)],
            send_sem=a_send.at[g],
            recv_sem=a_recv.at[g],
            device_id=(right, ch),
            device_id_type=MESH,
        )

    total_a = jnp.zeros((cart, 128), F32)
    total_b = jnp.zeros((cart, 128), F32)
    for g in range(groups):
        whole(g).wait_recv()
        at = slice(g * rows, (g + 1) * rows)
        total_a += jnp.dot(sa[:, at], arr[g], preferred_element_type=F32)
        total_b += jnp.dot(sb[:, at], arr[g], preferred_element_type=F32)

    half = cart // 2
    lane = lax.broadcasted_iota(jnp.int32, (half, 128), 1)
    first = total_a[:half] + pltpu.roll(total_b[:half], 64, 1)
    second = pltpu.roll(total_a[half:], 64, 1) + total_b[half:]
    rbuf[ch] = jnp.where(lane < 64, first, second).astype(BF)
    rcopies = []
    for d in range(1, 4):
        c = pltpu.make_async_remote_copy(
            src_ref=rbuf.at[ch],
            dst_ref=rbuf.at[ch],
            send_sem=r_send.at[d - 1],
            recv_sem=r_recv.at[d - 1],
            device_id=(az, lax.rem(ch + d, 4)),
            device_id_type=MESH,
        )
        c.start()
        rcopies.append(c)
    for c in rcopies:
        c.wait_recv()
    for p in range(2):
        sum_p = jnp.zeros((hh, half), F32)
        for g in range(4):
            sum_p += lax.dot_general(
                wx[p, :, g * 128 : (g + 1) * 128],
                rbuf[g],
                (((1,), (1,)), ((), ())),
                preferred_element_type=F32,
            )
        out[:, p * half : (p + 1) * half] = (sum_p + bias3).astype(BF)

    for c in e1 + e2 + wcopies + passed + rcopies + [c for k in range(4) for c in gathers[k]]:
        c.wait_send()

    @pl.when(ch == 0)
    def _():
        asked(rq, 0, share - 1, rq_send, rq_recv).wait_send()

    @pl.when(ch != 0)
    def _():
        asked(rq, 0, share, rq_send, rq_recv).wait_send()

    for g in range(groups):
        whole(g).wait_send()


def local(
    features,
    conv1_weight,
    conv1_bias,
    conv2_weight,
    conv2_bias,
    request_cell,
    corner_slot,
    corner_frac,
    expand_weight,
    expand_bias,
):
    n = lax.axis_size("az")
    chans, columns, ranges = features.shape
    outs = conv1_weight.shape[0]
    cart = corner_slot.shape[1]
    hh = expand_bias.shape[0]
    groups = torus(n)[0]
    members = n // groups
    rows = members * HALF

    w1 = conv1_weight.transpose(1, 2, 0, 3).reshape(9 * outs, chans)
    w2 = conv2_weight.transpose(1, 2, 0, 3).reshape(9 * outs, chans)
    args = (
        features,
        w1,
        conv1_bias.reshape(1, outs),
        w2,
        conv2_bias.reshape(1, outs),
        request_cell.reshape(n * 2 * HALF // 128, 1, 128),
        corner_slot,
        corner_frac,
        expand_weight,
        expand_bias.reshape(1, hh),
    )
    dma = pltpu.SemaphoreType.DMA
    return pl.pallas_call(
        functools.partial(kernel, n),
        out_shape=jax.ShapeDtypeStruct((hh, cart), BF),
        in_specs=[pl.BlockSpec(memory_space=pl.ANY)] * len(args),
        out_specs=pl.BlockSpec(memory_space=pltpu.VMEM),
        scratch_shapes=[
            pltpu.VMEM((chans, 4, ranges), BF),
            pltpu.VMEM((4 * chans, ranges), BF),
            pltpu.VMEM((9 * outs, chans), BF),
            pltpu.VMEM((1, outs), F32),
            pltpu.VMEM((9 * outs, chans), BF),
            pltpu.VMEM((1, outs), F32),
            pltpu.VMEM((n * 2 * HALF // 128, 1, 128), jnp.int32),
            pltpu.VMEM((4, cart), jnp.int32),
            pltpu.VMEM((2, cart), F32),
            pltpu.VMEM((1, hh), F32),
            pltpu.VMEM((4 * chans, ranges), BF),
            pltpu.VMEM((2, outs, ranges), BF),
            pltpu.VMEM((2, outs, ranges), BF),
            pltpu.VMEM((2, outs, ranges), BF),
            pltpu.VMEM((2, outs, ranges), BF),
            pltpu.VMEM((2, outs, ranges), F32),
            pltpu.VMEM((n * HALF, 4 * ranges), BF),
            pltpu.VMEM((n * HALF, 4 * ranges), BF),
            pltpu.VMEM((cart, n * HALF), BF),
            pltpu.VMEM((cart, n * HALF), BF),
            pltpu.VMEM((cart, 128), jnp.int32),
            pltpu.VMEM((cart, 128), F32),
            pltpu.VMEM((128, n), jnp.int32),
            pltpu.VMEM((groups, 2 * HALF, members), jnp.int32),
            pltpu.VMEM((groups, rows, 128), BF),
            pltpu.VMEM((groups, rows, 128), BF),
            pltpu.VMEM((2, 4 * ranges, 128), BF),
            pltpu.VMEM((n, 1, 128), jnp.int32),
            pltpu.VMEM((4, outs, hh), BF),
            pltpu.VMEM((2, hh, 512), BF),
            pltpu.VMEM((4, cart // 2, 128), BF),
            dma((10,)),
            dma((2,)),
            dma((2,)),
            dma((2,)),
            dma((2,)),
            dma,
            dma,
            dma((3,)),
            dma((3,)),
            dma((3,)),
            dma((3,)),
            dma((4, 3)),
            dma((4, 3)),
            dma((3,)),
            dma((3,)),
            dma((groups,)),
            dma((groups,)),
        ],
        compiler_params=pltpu.CompilerParams(
            collective_id=0, has_side_effects=True, vmem_limit_bytes=60 * 1024 * 1024
        ),
        cost_estimate=pl.CostEstimate(
            flops=4 * 10**9, bytes_accessed=2 * 10**6, transcendentals=0
        ),
    )(*args)


def solution(mesh):
    return jax.shard_map(
        local,
        mesh=mesh,
        in_specs=(
            P(None, "az", None),
            P("ch", None, None, None),
            P("ch"),
            P("ch", None, None, None),
            P("ch"),
            P("az"),
            P(None, "az"),
            P(None, "az"),
            P("ch", None),
            P("ch"),
        ),
        out_specs=P("ch", "az"),
        check_vma=False,
    )
```

```python
import functools

import jax
import jax.numpy as jnp
from jax import lax
from jax.experimental import pallas as pl
from jax.experimental.pallas import tpu as pltpu
from jax.sharding import PartitionSpec as P

MESH = pl.DeviceIdType.MESH
BF = jnp.bfloat16
F32 = jnp.float32
HALF = 16


def torus(n):
    return (8, 4, 4) if n == 128 else (2, 1, n // 2)


def combine(acc, rows, ranges):
    lane = lax.broadcasted_iota(jnp.int32, (rows, ranges), 1)
    low = jnp.where(lane == 0, 0.0, pltpu.roll(acc[:rows], 1, 1))
    high = jnp.where(lane == ranges - 1, 0.0, pltpu.roll(acc[2 * rows :], ranges - 1, 1))
    return low + acc[rows : 2 * rows] + high


def column_of(row):
    k = row.shape[1]
    a = lax.broadcasted_iota(jnp.int32, (k, k), 0)
    b = lax.broadcasted_iota(jnp.int32, (k, k), 1)
    return jnp.sum(jnp.where(a == b, jnp.broadcast_to(row, (k, k)), 0.0), axis=1, keepdims=True)


def kernel(
    n,
    feat,
    w1_in,
    b1_in,
    w2_in,
    b2_in,
    req_in,
    slot_in,
    frac_in,
    wexp,
    b3_in,
    out,
    fv,
    x1,
    w1,
    b1,
    w2,
    b2,
    req,
    slot,
    frac,
    b3,
    h1,
    e1s,
    e1r,
    e2s,
    e2r,
    acc_edge,
    oha,
    ohb,
    sa,
    sb,
    keyt,
    wt,
    reqt,
    reqg,
    pbuf,
    arr,
    h2t,
    rq,
    wr,
    wx,
    rbuf,
    in_sem,
    e1_send,
    e1_recv,
    e2_send,
    e2_recv,
    rq_send,
    rq_recv,
    rg_send,
    rg_recv,
    w_send,
    w_recv,
    g_send,
    g_recv,
    r_send,
    r_recv,
    a_send,
    a_recv,
):
    az = lax.axis_index("az")
    ch = lax.axis_index("ch")
    nz, nx, ny = torus(n)
    members = nx * ny
    groups = nz
    chans = x1.shape[0] // 4
    ranges = x1.shape[1]
    outs = w1.shape[0] // 9
    cart = slot.shape[1]
    rows = members * HALF
    hh = out.shape[0]
    share = n // 4
    right = lax.rem(az + 1, n)
    left = lax.rem(az + n - 1, n)
    my_z = az // members
    my_x = lax.rem(az, members) // ny
    my_y = lax.rem(az, ny)

    fetches = []
    pairs = (
        (feat, fv),
        (w1_in, w1),
        (req_in, req),
        (b1_in, b1),
        (w2_in, w2),
        (b2_in, b2),
        (slot_in, slot),
        (frac_in, frac),
        (b3_in, b3),
    )
    for k, (src, dst) in enumerate(pairs):
        c = pltpu.make_async_copy(src, dst, in_sem.at[k])
        c.start()
        fetches.append(c)

    side, core = ch // 2, lax.rem(ch, 2)
    peers = {
        1: side * 2 + 1 - core,
        2: (1 - side) * 2 + core,
        3: (1 - side) * 2 + 1 - core,
    }

    barrier = pltpu.get_barrier_semaphore()

    def hail(to_az, to_ch):
        pl.semaphore_signal(barrier, inc=1, device_id=(to_az, to_ch), device_id_type=MESH)

    hail(right, ch)
    hail(left, ch)
    for d in range(1, 4):
        hail(az, peers[d])

    def greet(d, _):
        to = az + d
        hail(jnp.where(to >= n, to - n, to), ch)
        return 0

    lax.fori_loop(2, n - 1, greet, 0, unroll=True)

    def at_column(col):
        return slice(col * chans, (col + 1) * chans)

    def part(w, x, col):
        total = None
        for tap in range(3):
            src = col + tap - 1
            if 0 <= src <= 3:
                term = jnp.dot(
                    w[tap * 3 * outs : (tap + 1) * 3 * outs, :],
                    x[at_column(src), :],
                    preferred_element_type=F32,
                )
                total = term if total is None else total + term
        return combine(total, outs, ranges)

    fetches[0].wait()
    for col in (3, 0):
        x1[at_column(col), :] = fv[:, col, :]
    fetches[1].wait()
    e1s[0] = part(w1, x1, 4).astype(BF)
    e1s[1] = part(w1, x1, -1).astype(BF)
    fetches[2].wait()

    pl.semaphore_wait(barrier, n + 2)

    def edge(src, dst, send, recv):
        copies = []
        for k, to in ((0, right), (1, left)):
            copies.append(
                pltpu.make_async_remote_copy(
                    src_ref=src.at[k],
                    dst_ref=dst.at[k],
                    send_sem=send.at[k],
                    recv_sem=recv.at[k],
                    device_id=(to, ch),
                    device_id_type=MESH,
                )
            )
        return copies

    e1 = edge(e1s, e1r, e1_send, e1_recv)
    for c in e1:
        c.start()

    def shifted(g, i, sign):
        dz = lax.rem(g + i, nz)
        dx = i // ny
        dy = lax.rem(i, ny)
        if sign > 0:
            z, x, y = my_z + dz, my_x + dx, my_y + dy
        else:
            z, x, y = my_z + nz - dz, my_x + nx - dx, my_y + ny - dy
        return lax.rem(z, nz) * members + lax.rem(x, nx) * ny + lax.rem(y, ny)

    def ask(k, _):
        p = ch * share + k
        to = shifted(p // members, lax.rem(p, members), -1)
        pltpu.make_async_remote_copy(
            src_ref=req.at[to // 4],
            dst_ref=rq.at[p],
            send_sem=rq_send,
            recv_sem=rq_recv,
            device_id=(to, ch),
            device_id_type=MESH,
        ).start()
        return 0

    @pl.when(ch == 0)
    def _():
        pltpu.make_async_copy(req.at[az // 4], rq.at[0], rq_recv).start()

    lax.fori_loop(jnp.where(ch == 0, 1, 0), share, ask, 0)

    wcopies = []
    for d in range(1, 4):
        to = peers[d]
        c = pltpu.make_async_remote_copy(
            src_ref=wexp.at[:, pl.ds(pl.multiple_of(to * hh, hh), hh)],
            dst_ref=wr.at[ch],
            send_sem=w_send.at[d - 1],
            recv_sem=w_recv.at[d - 1],
            device_id=(az, to),
            device_id_type=MESH,
        )
        c.start()
        wcopies.append(c)
    own_w = pltpu.make_async_copy(
        wexp.at[:, pl.ds(pl.multiple_of(ch * hh, hh), hh)], wr.at[ch], in_sem.at[len(pairs)]
    )
    own_w.start()

    for col in (1, 2):
        x1[at_column(col), :] = fv[:, col, :]
    fetches[3].wait()
    bias1 = column_of(b1[...])

    def mine(col):
        return pl.ds(pl.multiple_of(col * chans + ch * outs, outs), outs)

    def block_of(col, owner):
        return pl.ds(pl.multiple_of(col * chans + owner * outs, outs), outs)

    def pass_block(col, owner, to, lane):
        c = pltpu.make_async_remote_copy(
            src_ref=h1.at[block_of(col, owner)],
            dst_ref=h1.at[block_of(col, owner)],
            send_sem=g_send.at[col, lane - 1],
            recv_sem=g_recv.at[col, lane - 1],
            device_id=(az, peers[to]),
            device_id_type=MESH,
        )
        c.start()
        return c

    gathers = {}
    for col in (1, 2):
        h1[mine(col), :] = jnp.maximum(part(w1, x1, col) + bias1, 0.0).astype(BF)
        gathers[col] = [pass_block(col, ch, d, d) for d in (2, 1)]
    for k, col in ((1, 3), (0, 0)):
        acc_edge[k] = part(w1, x1, col) + bias1

    def asked(ref, at, count, send, recv):
        return pltpu.make_async_remote_copy(
            src_ref=ref.at[pl.ds(at, count)],
            dst_ref=ref.at[pl.ds(at, count)],
            send_sem=send,
            recv_sem=recv,
            device_id=(right, ch),
            device_id_type=MESH,
        )

    for k, col in ((1, 3), (0, 0)):
        e1[k].wait_recv()
        h1[mine(col), :] = jnp.maximum(acc_edge[k] + e1r[k].astype(F32), 0.0).astype(BF)
        gathers[col] = [pass_block(col, ch, d, d) for d in (3, 2, 1)]
    for col in (1, 2):
        gathers[col][0].wait_recv()
        gathers[col].append(pass_block(col, peers[2], 1, 3))

    asked(rq, 0, share, rq_send, rq_recv).wait_recv()
    passed = []
    for d in range(1, 4):
        at = pl.ds(pl.multiple_of(ch * share, share), share)
        c = pltpu.make_async_remote_copy(
            src_ref=rq.at[at],
            dst_ref=rq.at[at],
            send_sem=rg_send.at[d - 1],
            recv_sem=rg_recv.at[d - 1],
            device_id=(az, peers[d]),
            device_id_type=MESH,
        )
        c.start()
        passed.append(c)

    for c in fetches[4:]:
        c.wait()
    q = slot[...]
    sector = lax.shift_right_logical(q, 5)
    low = jnp.bitwise_and(q, HALF - 1)
    upper = jnp.bitwise_and(q, HALF) != 0
    dx = jnp.bitwise_and(my_x - jnp.bitwise_and(sector // ny, nx - 1), nx - 1)
    dy = jnp.bitwise_and(my_y - jnp.bitwise_and(sector, ny - 1), ny - 1)
    place_i = dx * ny + dy
    place_g = jnp.bitwise_and(my_z - sector // members - place_i, nz - 1)
    m = (place_g * members + place_i) * HALF + low
    keys = jnp.concatenate(
        [jnp.where(upper, -1, m), jnp.where(upper, m, -1)]
        + [jnp.zeros((120, cart), jnp.int32)],
        axis=0,
    )
    keyt[...] = keys.T
    u, v = frac[0:1, :], frac[1:2, :]
    weights = jnp.concatenate(
        [(1.0 - u) * (1.0 - v), u * (1.0 - v), (1.0 - u) * v, u * v]
        + [jnp.zeros((124, cart), F32)],
        axis=0,
    )
    wt[...] = weights.T
    width = min(128, n * HALF)

    def s_rows(b, _):
        at = pl.ds(pl.multiple_of(b * 16, 16), 16)
        spot = lax.broadcasted_iota(jnp.int32, (16, width), 1).astype(jnp.int16)
        parts = [jnp.broadcast_to(wt[at, k : k + 1], (16, width)).astype(BF) for k in range(4)]
        for base, ref in ((0, sa), (4, sb)):
            found = [
                jnp.broadcast_to(keyt[at, base + k : base + k + 1], (16, width)).astype(jnp.int16)
                for k in range(4)
            ]
            for j in range(n * HALF // width):
                here = spot + jnp.int16(j * width)
                total = jnp.zeros((16, width), BF)
                for k in range(4):
                    total = jnp.where(here == found[k], parts[k], total)
                ref[at, j * width : (j + 1) * width] = total
        return 0

    lax.fori_loop(0, cart // 16, s_rows, 0, unroll=2 if cart >= 32 else 1)

    e2 = edge(e2s, e2r, e2_send, e2_recv)
    for k, col, to in ((0, 3, 4), (1, 0, -1)):
        for c in gathers[col]:
            c.wait_recv()
        e2s[k] = part(w2, h1, to).astype(BF)
        e2[k].start()
    gathers[1][1].wait_recv()
    gathers[1][2].wait_recv()
    gathers[2][1].wait_recv()
    gathers[2][2].wait_recv()

    def place(col, value):
        zero = jnp.zeros((128 - outs, ranges), F32)
        at = slice(col * ranges, (col + 1) * ranges)
        h2t[0, at, :] = jnp.concatenate([value, zero], axis=0).T.astype(BF)
        h2t[1, at, :] = jnp.concatenate([zero, value], axis=0).T.astype(BF)

    bias2 = column_of(b2[...])
    for col in (1, 2):
        place(col, jnp.maximum(part(w2, h1, col) + bias2, 0.0))
    for k, col in ((0, 0), (1, 3)):
        acc_edge[k] = part(w2, h1, col) + bias2

    for c in passed:
        c.wait_recv()
    reqt[...] = rq[:, 0, :].T
    wanted = reqt[pl.ds(pl.multiple_of(lax.rem(az, 4) * 2 * HALF, 2 * HALF), 2 * HALF), :]
    for g in range(groups):
        reqg[g] = wanted[:, g * members : (g + 1) * members]

    def one_hot(g, _):
        some = reqg[g]
        spot = lax.broadcasted_iota(jnp.int32, (HALF, 4 * ranges), 1)
        for i in range(members):
            at = pl.ds(pl.multiple_of(g * rows + i * HALF, HALF), HALF)
            oha[at, :] = jnp.where(spot == some[:HALF, i : i + 1], 1.0, 0.0).astype(BF)
            ohb[at, :] = jnp.where(spot == some[HALF:, i : i + 1], 1.0, 0.0).astype(BF)
        return 0

    lax.fori_loop(0, groups, one_hot, 0)

    own_w.wait()
    for d in range(3):
        wcopies[d].wait_recv()
    for g in range(4):
        block = wr[g].astype(F32)
        zero = jnp.zeros((128 - outs, hh), F32)
        wx[0, :, g * 128 : (g + 1) * 128] = jnp.concatenate([block, zero], axis=0).T.astype(BF)
        wx[1, :, g * 128 : (g + 1) * 128] = jnp.concatenate([zero, block], axis=0).T.astype(BF)
    bias3 = column_of(b3[...])

    for k, col in ((0, 0), (1, 3)):
        e2[k].wait_recv()
        place(col, jnp.maximum(acc_edge[k] + e2r[k].astype(F32), 0.0))

    for g in range(groups):
        at = slice(g * rows, (g + 1) * rows)
        picked = jnp.dot(oha[at, :], h2t[0], preferred_element_type=F32)
        picked += jnp.dot(ohb[at, :], h2t[1], preferred_element_type=F32)
        pbuf[g] = picked.astype(BF)

        def ship(i, _):
            block = pl.ds(pl.multiple_of(i * HALF, HALF), HALF)
            pltpu.make_async_remote_copy(
                src_ref=pbuf.at[g, block],
                dst_ref=arr.at[g, block],
                send_sem=a_send.at[g],
                recv_sem=a_recv.at[g],
                device_id=(shifted(g, i, 1), ch),
                device_id_type=MESH,
            ).start()
            return 0

        lax.fori_loop(1 if g == 0 else 0, members, ship, 0)
        if g == 0:
            arr[0, :HALF, :] = pbuf[0, :HALF, :]

    def whole(g):
        size = rows - HALF if g == 0 else rows
        return pltpu.make_async_remote_copy(
            src_ref=pbuf.at[g, pl.ds(0, size)],
            dst_ref=arr.at[g, pl.ds(0, size)],
            send_sem=a_send.at[g],
            recv_sem=a_recv.at[g],
            device_id=(right, ch),
            device_id_type=MESH,
        )

    total_a = jnp.zeros((cart, 128), F32)
    total_b = jnp.zeros((cart, 128), F32)
    for g in range(groups):
        whole(g).wait_recv()
        at = slice(g * rows, (g + 1) * rows)
        total_a += jnp.dot(sa[:, at], arr[g], preferred_element_type=F32)
        total_b += jnp.dot(sb[:, at], arr[g], preferred_element_type=F32)

    half = cart // 2
    lane = lax.broadcasted_iota(jnp.int32, (half, 128), 1)
    first = total_a[:half] + pltpu.roll(total_b[:half], 64, 1)
    second = pltpu.roll(total_a[half:], 64, 1) + total_b[half:]
    rbuf[ch] = jnp.where(lane < 64, first, second).astype(BF)
    rcopies = []
    for d in range(1, 4):
        c = pltpu.make_async_remote_copy(
            src_ref=rbuf.at[ch],
            dst_ref=rbuf.at[ch],
            send_sem=r_send.at[d - 1],
            recv_sem=r_recv.at[d - 1],
            device_id=(az, peers[d]),
            device_id_type=MESH,
        )
        c.start()
        rcopies.append(c)
    for c in rcopies:
        c.wait_recv()
    for p in range(2):
        sum_p = jnp.zeros((hh, half), F32)
        for g in range(4):
            sum_p += lax.dot_general(
                wx[p, :, g * 128 : (g + 1) * 128],
                rbuf[g],
                (((1,), (1,)), ((), ())),
                preferred_element_type=F32,
            )
        out[:, p * half : (p + 1) * half] = (sum_p + bias3).astype(BF)

    for c in e1 + e2 + wcopies + passed + rcopies + [c for k in range(4) for c in gathers[k]]:
        c.wait_send()

    @pl.when(ch == 0)
    def _():
        asked(rq, 0, share - 1, rq_send, rq_recv).wait_send()

    @pl.when(ch != 0)
    def _():
        asked(rq, 0, share, rq_send, rq_recv).wait_send()

    for g in range(groups):
        whole(g).wait_send()


def local(
    features,
    conv1_weight,
    conv1_bias,
    conv2_weight,
    conv2_bias,
    request_cell,
    corner_slot,
    corner_frac,
    expand_weight,
    expand_bias,
):
    n = lax.axis_size("az")
    chans, columns, ranges = features.shape
    outs = conv1_weight.shape[0]
    cart = corner_slot.shape[1]
    hh = expand_bias.shape[0]
    groups = torus(n)[0]
    members = n // groups
    rows = members * HALF

    w1 = conv1_weight.transpose(1, 2, 0, 3).reshape(9 * outs, chans)
    w2 = conv2_weight.transpose(1, 2, 0, 3).reshape(9 * outs, chans)
    args = (
        features,
        w1,
        conv1_bias.reshape(1, outs),
        w2,
        conv2_bias.reshape(1, outs),
        request_cell.reshape(n * 2 * HALF // 128, 1, 128),
        corner_slot,
        corner_frac,
        expand_weight,
        expand_bias.reshape(1, hh),
    )
    dma = pltpu.SemaphoreType.DMA
    return pl.pallas_call(
        functools.partial(kernel, n),
        out_shape=jax.ShapeDtypeStruct((hh, cart), BF),
        in_specs=[pl.BlockSpec(memory_space=pl.ANY)] * len(args),
        out_specs=pl.BlockSpec(memory_space=pltpu.VMEM),
        scratch_shapes=[
            pltpu.VMEM((chans, 4, ranges), BF),
            pltpu.VMEM((4 * chans, ranges), BF),
            pltpu.VMEM((9 * outs, chans), BF),
            pltpu.VMEM((1, outs), F32),
            pltpu.VMEM((9 * outs, chans), BF),
            pltpu.VMEM((1, outs), F32),
            pltpu.VMEM((n * 2 * HALF // 128, 1, 128), jnp.int32),
            pltpu.VMEM((4, cart), jnp.int32),
            pltpu.VMEM((2, cart), F32),
            pltpu.VMEM((1, hh), F32),
            pltpu.VMEM((4 * chans, ranges), BF),
            pltpu.VMEM((2, outs, ranges), BF),
            pltpu.VMEM((2, outs, ranges), BF),
            pltpu.VMEM((2, outs, ranges), BF),
            pltpu.VMEM((2, outs, ranges), BF),
            pltpu.VMEM((2, outs, ranges), F32),
            pltpu.VMEM((n * HALF, 4 * ranges), BF),
            pltpu.VMEM((n * HALF, 4 * ranges), BF),
            pltpu.VMEM((cart, n * HALF), BF),
            pltpu.VMEM((cart, n * HALF), BF),
            pltpu.VMEM((cart, 128), jnp.int32),
            pltpu.VMEM((cart, 128), F32),
            pltpu.VMEM((128, n), jnp.int32),
            pltpu.VMEM((groups, 2 * HALF, members), jnp.int32),
            pltpu.VMEM((groups, rows, 128), BF),
            pltpu.VMEM((groups, rows, 128), BF),
            pltpu.VMEM((2, 4 * ranges, 128), BF),
            pltpu.VMEM((n, 1, 128), jnp.int32),
            pltpu.VMEM((4, outs, hh), BF),
            pltpu.VMEM((2, hh, 512), BF),
            pltpu.VMEM((4, cart // 2, 128), BF),
            dma((10,)),
            dma((2,)),
            dma((2,)),
            dma((2,)),
            dma((2,)),
            dma,
            dma,
            dma((3,)),
            dma((3,)),
            dma((3,)),
            dma((3,)),
            dma((4, 3)),
            dma((4, 3)),
            dma((3,)),
            dma((3,)),
            dma((groups,)),
            dma((groups,)),
        ],
        compiler_params=pltpu.CompilerParams(
            collective_id=0, has_side_effects=True, vmem_limit_bytes=60 * 1024 * 1024
        ),
        cost_estimate=pl.CostEstimate(
            flops=4 * 10**9, bytes_accessed=2 * 10**6, transcendentals=0
        ),
    )(*args)


def solution(mesh):
    return jax.shard_map(
        local,
        mesh=mesh,
        in_specs=(
            P(None, "az", None),
            P("ch", None, None, None),
            P("ch"),
            P("ch", None, None, None),
            P("ch"),
            P("az"),
            P(None, "az"),
            P(None, "az"),
            P("ch", None),
            P("ch"),
        ),
        out_specs=P("ch", "az"),
        check_vma=False,
    )
```

```python
import functools

import jax
import jax.numpy as jnp
from jax import lax
from jax.experimental import pallas as pl
from jax.experimental.pallas import tpu as pltpu
from jax.sharding import PartitionSpec as P

MESH = pl.DeviceIdType.MESH
BF = jnp.bfloat16
F32 = jnp.float32
HALF = 16


def torus(n):
    return (8, 4, 4) if n == 128 else (2, 1, n // 2)


def combine(acc, rows, ranges):
    lane = lax.broadcasted_iota(jnp.int32, (rows, ranges), 1)
    low = jnp.where(lane == 0, 0.0, pltpu.roll(acc[:rows], 1, 1))
    high = jnp.where(lane == ranges - 1, 0.0, pltpu.roll(acc[2 * rows :], ranges - 1, 1))
    return low + acc[rows : 2 * rows] + high


def column_of(row):
    k = row.shape[1]
    a = lax.broadcasted_iota(jnp.int32, (k, k), 0)
    b = lax.broadcasted_iota(jnp.int32, (k, k), 1)
    return jnp.sum(jnp.where(a == b, jnp.broadcast_to(row, (k, k)), 0.0), axis=1, keepdims=True)


def kernel(
    n,
    feat,
    w1_in,
    b1_in,
    w2_in,
    b2_in,
    req_in,
    slot_in,
    frac_in,
    wexp,
    b3_in,
    out,
    fv,
    x1,
    w1,
    b1,
    w2,
    b2,
    req,
    slot,
    frac,
    b3,
    h1,
    e1s,
    e1r,
    e2s,
    e2r,
    acc_edge,
    oha,
    ohb,
    sa,
    sb,
    keyt,
    wt,
    reqt,
    reqg,
    pbuf,
    arr,
    h2t,
    rq,
    wr,
    wx,
    rbuf,
    in_sem,
    e1_send,
    e1_recv,
    e2_send,
    e2_recv,
    rq_send,
    rq_recv,
    rg_send,
    rg_recv,
    w_send,
    w_recv,
    g_send,
    g_recv,
    r_send,
    r_recv,
    a_send,
    a_recv,
):
    az = lax.axis_index("az")
    ch = lax.axis_index("ch")
    nz, nx, ny = torus(n)
    members = nx * ny
    groups = nz
    chans = x1.shape[0] // 4
    ranges = x1.shape[1]
    outs = w1.shape[0] // 9
    cart = slot.shape[1]
    rows = members * HALF
    hh = out.shape[0]
    share = n // 4
    right = lax.rem(az + 1, n)
    left = lax.rem(az + n - 1, n)
    my_z = az // members
    my_x = lax.rem(az, members) // ny
    my_y = lax.rem(az, ny)

    fetches = []
    pairs = (
        (feat, fv),
        (w1_in, w1),
        (req_in, req),
        (b1_in, b1),
        (w2_in, w2),
        (b2_in, b2),
        (slot_in, slot),
        (frac_in, frac),
        (b3_in, b3),
    )
    for k, (src, dst) in enumerate(pairs):
        c = pltpu.make_async_copy(src, dst, in_sem.at[k])
        c.start()
        fetches.append(c)

    side, core = ch // 2, lax.rem(ch, 2)
    peers = {
        1: side * 2 + 1 - core,
        2: (1 - side) * 2 + core,
        3: (1 - side) * 2 + 1 - core,
    }

    barrier = pltpu.get_barrier_semaphore()

    def hail(to_az, to_ch):
        pl.semaphore_signal(barrier, inc=1, device_id=(to_az, to_ch), device_id_type=MESH)

    hail(right, ch)
    hail(left, ch)
    for d in range(1, 4):
        hail(az, peers[d])

    def greet(d, _):
        to = az + d
        hail(jnp.where(to >= n, to - n, to), ch)
        return 0

    lax.fori_loop(2, n - 1, greet, 0, unroll=True)

    def at_column(col):
        return slice(col * chans, (col + 1) * chans)

    def part(w, x, col):
        total = None
        for tap in range(3):
            src = col + tap - 1
            if 0 <= src <= 3:
                term = jnp.dot(
                    w[tap * 3 * outs : (tap + 1) * 3 * outs, :],
                    x[at_column(src), :],
                    preferred_element_type=F32,
                )
                total = term if total is None else total + term
        return combine(total, outs, ranges)

    fetches[0].wait()
    for col in (3, 0):
        x1[at_column(col), :] = fv[:, col, :]
    fetches[1].wait()
    e1s[0] = part(w1, x1, 4).astype(BF)
    e1s[1] = part(w1, x1, -1).astype(BF)
    fetches[2].wait()

    pl.semaphore_wait(barrier, n + 2)

    def edge(src, dst, send, recv):
        copies = []
        for k, to in ((0, right), (1, left)):
            copies.append(
                pltpu.make_async_remote_copy(
                    src_ref=src.at[k],
                    dst_ref=dst.at[k],
                    send_sem=send.at[k],
                    recv_sem=recv.at[k],
                    device_id=(to, ch),
                    device_id_type=MESH,
                )
            )
        return copies

    e1 = edge(e1s, e1r, e1_send, e1_recv)
    for c in e1:
        c.start()

    ahead_z = [lax.rem(my_z + d, nz) * members for d in range(nz)]
    back_z = [lax.rem(my_z + nz - d, nz) * members for d in range(nz)]
    ahead_xy, back_xy = [], []
    for i in range(members):
        ix, iy = i // ny, i % ny
        ahead_xy.append(lax.rem(my_x + ix, nx) * ny + lax.rem(my_y + iy, ny))
        back_xy.append(lax.rem(my_x + nx - ix, nx) * ny + lax.rem(my_y + ny - iy, ny))

    def ask(k):
        p = ch * share + k
        g = p // members
        i = lax.rem(p, members) if share % members else k % members
        if share % members:
            ix, iy = i // ny, lax.rem(i, ny)
            xy = lax.rem(my_x + nx - ix, nx) * ny + lax.rem(my_y + ny - iy, ny)
        else:
            xy = back_xy[i]
        to = lax.rem(my_z + nz - lax.rem(g + i, nz), nz) * members + xy
        pltpu.make_async_remote_copy(
            src_ref=req.at[to // 4],
            dst_ref=rq.at[p],
            send_sem=rq_send,
            recv_sem=rq_recv,
            device_id=(to, ch),
            device_id_type=MESH,
        ).start()

    wcopies = []
    for d in range(1, 4):
        to = peers[d]
        c = pltpu.make_async_remote_copy(
            src_ref=wexp.at[:, pl.ds(pl.multiple_of(to * hh, hh), hh)],
            dst_ref=wr.at[ch],
            send_sem=w_send.at[d - 1],
            recv_sem=w_recv.at[d - 1],
            device_id=(az, to),
            device_id_type=MESH,
        )
        c.start()
        wcopies.append(c)
    own_w = pltpu.make_async_copy(
        wexp.at[:, pl.ds(pl.multiple_of(ch * hh, hh), hh)], wr.at[ch], in_sem.at[len(pairs)]
    )
    own_w.start()

    @pl.when(ch == 0)
    def _():
        pltpu.make_async_copy(req.at[az // 4], rq.at[0], rq_recv).start()

    @pl.when(ch != 0)
    def _():
        ask(0)

    for k in range(1, share):
        ask(k)

    for col in (1, 2):
        x1[at_column(col), :] = fv[:, col, :]
    fetches[3].wait()
    bias1 = column_of(b1[...])

    def mine(col):
        return pl.ds(pl.multiple_of(col * chans + ch * outs, outs), outs)

    def block_of(col, owner):
        return pl.ds(pl.multiple_of(col * chans + owner * outs, outs), outs)

    def pass_block(col, owner, to, lane):
        c = pltpu.make_async_remote_copy(
            src_ref=h1.at[block_of(col, owner)],
            dst_ref=h1.at[block_of(col, owner)],
            send_sem=g_send.at[col, lane - 1],
            recv_sem=g_recv.at[col, lane - 1],
            device_id=(az, peers[to]),
            device_id_type=MESH,
        )
        c.start()
        return c

    gathers = {}
    for col in (1, 2):
        h1[mine(col), :] = jnp.maximum(part(w1, x1, col) + bias1, 0.0).astype(BF)
        gathers[col] = [pass_block(col, ch, d, d) for d in (2, 1)]
    for k, col in ((1, 3), (0, 0)):
        acc_edge[k] = part(w1, x1, col) + bias1

    def asked(ref, at, count, send, recv):
        return pltpu.make_async_remote_copy(
            src_ref=ref.at[pl.ds(at, count)],
            dst_ref=ref.at[pl.ds(at, count)],
            send_sem=send,
            recv_sem=recv,
            device_id=(right, ch),
            device_id_type=MESH,
        )

    for k, col in ((1, 3), (0, 0)):
        e1[k].wait_recv()
        h1[mine(col), :] = jnp.maximum(acc_edge[k] + e1r[k].astype(F32), 0.0).astype(BF)
        gathers[col] = [pass_block(col, ch, d, d) for d in (3, 2, 1)]
    for col in (1, 2):
        gathers[col][0].wait_recv()
        gathers[col].append(pass_block(col, peers[2], 1, 3))

    own_w.wait()
    for d in range(3):
        wcopies[d].wait_recv()
    for g in range(4):
        block = wr[g].astype(F32)
        zero = jnp.zeros((128 - outs, hh), F32)
        wx[0, :, g * 128 : (g + 1) * 128] = jnp.concatenate([block, zero], axis=0).T.astype(BF)
        wx[1, :, g * 128 : (g + 1) * 128] = jnp.concatenate([zero, block], axis=0).T.astype(BF)
    for k in (4, 5, 8):
        fetches[k].wait()
    bias2 = column_of(b2[...])
    bias3 = column_of(b3[...])

    asked(rq, 0, share, rq_send, rq_recv).wait_recv()
    passed = []
    for d in range(1, 4):
        at = pl.ds(pl.multiple_of(ch * share, share), share)
        c = pltpu.make_async_remote_copy(
            src_ref=rq.at[at],
            dst_ref=rq.at[at],
            send_sem=rg_send.at[d - 1],
            recv_sem=rg_recv.at[d - 1],
            device_id=(az, peers[d]),
            device_id_type=MESH,
        )
        c.start()
        passed.append(c)

    e2 = edge(e2s, e2r, e2_send, e2_recv)
    for k, col, to in ((0, 3, 4), (1, 0, -1)):
        for c in gathers[col]:
            c.wait_recv()
        e2s[k] = part(w2, h1, to).astype(BF)
        e2[k].start()
    gathers[1][1].wait_recv()
    gathers[1][2].wait_recv()
    gathers[2][1].wait_recv()
    gathers[2][2].wait_recv()

    def place(col, value):
        zero = jnp.zeros((128 - outs, ranges), F32)
        at = slice(col * ranges, (col + 1) * ranges)
        h2t[0, at, :] = jnp.concatenate([value, zero], axis=0).T.astype(BF)
        h2t[1, at, :] = jnp.concatenate([zero, value], axis=0).T.astype(BF)

    for col in (1, 2):
        place(col, jnp.maximum(part(w2, h1, col) + bias2, 0.0))
    for k, col in ((0, 0), (1, 3)):
        acc_edge[k] = part(w2, h1, col) + bias2

    for c in passed:
        c.wait_recv()
    reqt[...] = rq[:, 0, :].T
    wanted = reqt[pl.ds(pl.multiple_of(lax.rem(az, 4) * 2 * HALF, 2 * HALF), 2 * HALF), :]
    for g in range(groups):
        reqg[g] = wanted[:, g * members : (g + 1) * members]

    def one_hot(g, _):
        some = reqg[g]
        spot = lax.broadcasted_iota(jnp.int32, (HALF, 4 * ranges), 1)
        for i in range(members):
            at = pl.ds(pl.multiple_of(g * rows + i * HALF, HALF), HALF)
            oha[at, :] = jnp.where(spot == some[:HALF, i : i + 1], 1.0, 0.0).astype(BF)
            ohb[at, :] = jnp.where(spot == some[HALF:, i : i + 1], 1.0, 0.0).astype(BF)
        return 0

    lax.fori_loop(0, groups, one_hot, 0)

    for k, col in ((0, 0), (1, 3)):
        e2[k].wait_recv()
        place(col, jnp.maximum(acc_edge[k] + e2r[k].astype(F32), 0.0))

    for g in range(groups):
        at = slice(g * rows, (g + 1) * rows)
        picked = jnp.dot(oha[at, :], h2t[0], preferred_element_type=F32)
        picked += jnp.dot(ohb[at, :], h2t[1], preferred_element_type=F32)
        pbuf[g] = picked.astype(BF)

        for i in range(1 if g == 0 else 0, members):
            block = slice(i * HALF, (i + 1) * HALF)
            pltpu.make_async_remote_copy(
                src_ref=pbuf.at[g, block],
                dst_ref=arr.at[g, block],
                send_sem=a_send.at[g],
                recv_sem=a_recv.at[g],
                device_id=(ahead_z[(g + i) % nz] + ahead_xy[i], ch),
                device_id_type=MESH,
            ).start()
        if g == 0:
            arr[0, :HALF, :] = pbuf[0, :HALF, :]

    fetches[6].wait()
    fetches[7].wait()
    q = slot[...]
    sector = lax.shift_right_logical(q, 5)
    low = jnp.bitwise_and(q, HALF - 1)
    upper = jnp.bitwise_and(q, HALF) != 0
    dx = jnp.bitwise_and(my_x - jnp.bitwise_and(sector // ny, nx - 1), nx - 1)
    dy = jnp.bitwise_and(my_y - jnp.bitwise_and(sector, ny - 1), ny - 1)
    place_i = dx * ny + dy
    place_g = jnp.bitwise_and(my_z - sector // members - place_i, nz - 1)
    m = (place_g * members + place_i) * HALF + low
    keys = jnp.concatenate(
        [jnp.where(upper, -1, m), jnp.where(upper, m, -1)]
        + [jnp.zeros((120, cart), jnp.int32)],
        axis=0,
    )
    keyt[...] = keys.T
    u, v = frac[0:1, :], frac[1:2, :]
    weights = jnp.concatenate(
        [(1.0 - u) * (1.0 - v), u * (1.0 - v), (1.0 - u) * v, u * v]
        + [jnp.zeros((124, cart), F32)],
        axis=0,
    )
    wt[...] = weights.T
    width = min(128, n * HALF)

    def s_rows(b, _):
        at = pl.ds(pl.multiple_of(b * 16, 16), 16)
        spot = lax.broadcasted_iota(jnp.int32, (16, width), 1).astype(jnp.int16)
        parts = [jnp.broadcast_to(wt[at, k : k + 1], (16, width)).astype(BF) for k in range(4)]
        for base, ref in ((0, sa), (4, sb)):
            found = [
                jnp.broadcast_to(keyt[at, base + k : base + k + 1], (16, width)).astype(jnp.int16)
                for k in range(4)
            ]
            for j in range(n * HALF // width):
                here = spot + jnp.int16(j * width)
                total = jnp.zeros((16, width), BF)
                for k in range(4):
                    total = jnp.where(here == found[k], parts[k], total)
                ref[at, j * width : (j + 1) * width] = total
        return 0

    lax.fori_loop(0, cart // 16, s_rows, 0, unroll=2 if cart >= 32 else 1)

    def whole(g):
        size = rows - HALF if g == 0 else rows
        return pltpu.make_async_remote_copy(
            src_ref=pbuf.at[g, pl.ds(0, size)],
            dst_ref=arr.at[g, pl.ds(0, size)],
            send_sem=a_send.at[g],
            recv_sem=a_recv.at[g],
            device_id=(right, ch),
            device_id_type=MESH,
        )

    half = cart // 2
    piece = half // 2
    sums = {}
    for g in range(groups):
        whole(g).wait_recv()
        at = slice(g * rows, (g + 1) * rows)
        for h in range(2):
            for p in range(2):
                cells = slice(p * half + h * piece, p * half + (h + 1) * piece)
                for name, ref in (("a", sa), ("b", sb)):
                    term = jnp.dot(ref[cells, at], arr[g], preferred_element_type=F32)
                    key = (h, p, name)
                    sums[key] = term if g == 0 else sums[key] + term
    lane = lax.broadcasted_iota(jnp.int32, (piece, 128), 1)
    rcopies = {}
    for h in range(2):
        first = sums[h, 0, "a"] + pltpu.roll(sums[h, 0, "b"], 64, 1)
        second = pltpu.roll(sums[h, 1, "a"], 64, 1) + sums[h, 1, "b"]
        at = slice(h * piece, (h + 1) * piece)
        rbuf[ch, at, :] = jnp.where(lane < 64, first, second).astype(BF)
        rcopies[h] = []
        for d in (3, 2, 1):
            c = pltpu.make_async_remote_copy(
                src_ref=rbuf.at[ch, at],
                dst_ref=rbuf.at[ch, at],
                send_sem=r_send.at[h, d - 1],
                recv_sem=r_recv.at[h, d - 1],
                device_id=(az, peers[d]),
                device_id_type=MESH,
            )
            c.start()
            rcopies[h].append(c)
    for h in range(2):
        for c in rcopies[h]:
            c.wait_recv()
        at = slice(h * piece, (h + 1) * piece)
        for p in range(2):
            sum_p = jnp.zeros((hh, piece), F32)
            for g in range(4):
                sum_p += lax.dot_general(
                    wx[p, :, g * 128 : (g + 1) * 128],
                    rbuf[g, at, :],
                    (((1,), (1,)), ((), ())),
                    preferred_element_type=F32,
                )
            cells = slice(p * half + h * piece, p * half + (h + 1) * piece)
            out[:, cells] = (sum_p + bias3).astype(BF)

    for c in e1 + e2 + wcopies + passed + rcopies[0] + rcopies[1] + [c for k in range(4) for c in gathers[k]]:
        c.wait_send()

    @pl.when(ch == 0)
    def _():
        asked(rq, 0, share - 1, rq_send, rq_recv).wait_send()

    @pl.when(ch != 0)
    def _():
        asked(rq, 0, share, rq_send, rq_recv).wait_send()

    for g in range(groups):
        whole(g).wait_send()


def local(
    features,
    conv1_weight,
    conv1_bias,
    conv2_weight,
    conv2_bias,
    request_cell,
    corner_slot,
    corner_frac,
    expand_weight,
    expand_bias,
):
    n = lax.axis_size("az")
    chans, columns, ranges = features.shape
    outs = conv1_weight.shape[0]
    cart = corner_slot.shape[1]
    hh = expand_bias.shape[0]
    groups = torus(n)[0]
    members = n // groups
    rows = members * HALF

    w1 = conv1_weight.transpose(1, 2, 0, 3).reshape(9 * outs, chans)
    w2 = conv2_weight.transpose(1, 2, 0, 3).reshape(9 * outs, chans)
    args = (
        features,
        w1,
        conv1_bias.reshape(1, outs),
        w2,
        conv2_bias.reshape(1, outs),
        request_cell.reshape(n * 2 * HALF // 128, 1, 128),
        corner_slot,
        corner_frac,
        expand_weight,
        expand_bias.reshape(1, hh),
    )
    dma = pltpu.SemaphoreType.DMA
    return pl.pallas_call(
        functools.partial(kernel, n),
        out_shape=jax.ShapeDtypeStruct((hh, cart), BF),
        in_specs=[pl.BlockSpec(memory_space=pl.ANY)] * len(args),
        out_specs=pl.BlockSpec(memory_space=pltpu.VMEM),
        scratch_shapes=[
            pltpu.VMEM((chans, 4, ranges), BF),
            pltpu.VMEM((4 * chans, ranges), BF),
            pltpu.VMEM((9 * outs, chans), BF),
            pltpu.VMEM((1, outs), F32),
            pltpu.VMEM((9 * outs, chans), BF),
            pltpu.VMEM((1, outs), F32),
            pltpu.VMEM((n * 2 * HALF // 128, 1, 128), jnp.int32),
            pltpu.VMEM((4, cart), jnp.int32),
            pltpu.VMEM((2, cart), F32),
            pltpu.VMEM((1, hh), F32),
            pltpu.VMEM((4 * chans, ranges), BF),
            pltpu.VMEM((2, outs, ranges), BF),
            pltpu.VMEM((2, outs, ranges), BF),
            pltpu.VMEM((2, outs, ranges), BF),
            pltpu.VMEM((2, outs, ranges), BF),
            pltpu.VMEM((2, outs, ranges), F32),
            pltpu.VMEM((n * HALF, 4 * ranges), BF),
            pltpu.VMEM((n * HALF, 4 * ranges), BF),
            pltpu.VMEM((cart, n * HALF), BF),
            pltpu.VMEM((cart, n * HALF), BF),
            pltpu.VMEM((cart, 128), jnp.int32),
            pltpu.VMEM((cart, 128), F32),
            pltpu.VMEM((128, n), jnp.int32),
            pltpu.VMEM((groups, 2 * HALF, members), jnp.int32),
            pltpu.VMEM((groups, rows, 128), BF),
            pltpu.VMEM((groups, rows, 128), BF),
            pltpu.VMEM((2, 4 * ranges, 128), BF),
            pltpu.VMEM((n, 1, 128), jnp.int32),
            pltpu.VMEM((4, outs, hh), BF),
            pltpu.VMEM((2, hh, 512), BF),
            pltpu.VMEM((4, cart // 2, 128), BF),
            dma((10,)),
            dma((2,)),
            dma((2,)),
            dma((2,)),
            dma((2,)),
            dma,
            dma,
            dma((3,)),
            dma((3,)),
            dma((3,)),
            dma((3,)),
            dma((4, 3)),
            dma((4, 3)),
            dma((2, 3)),
            dma((2, 3)),
            dma((groups,)),
            dma((groups,)),
        ],
        compiler_params=pltpu.CompilerParams(
            collective_id=0, has_side_effects=True, vmem_limit_bytes=48 * 1024 * 1024
        ),
        cost_estimate=pl.CostEstimate(
            flops=4 * 10**9, bytes_accessed=2 * 10**6, transcendentals=0
        ),
    )(*[pltpu.with_memory_space_constraint(x, pltpu.HBM) for x in args])


def solution(mesh):
    return jax.shard_map(
        local,
        mesh=mesh,
        in_specs=(
            P(None, "az", None),
            P("ch", None, None, None),
            P("ch"),
            P("ch", None, None, None),
            P("ch"),
            P("az"),
            P(None, "az"),
            P(None, "az"),
            P("ch", None),
            P("ch"),
        ),
        out_specs=P("ch", "az"),
        check_vma=False,
    )
```

```python
import functools

import jax
import jax.numpy as jnp
from jax import lax
from jax.experimental import pallas as pl
from jax.experimental.pallas import tpu as pltpu
from jax.sharding import PartitionSpec as P

MESH = pl.DeviceIdType.MESH
BF = jnp.bfloat16
F32 = jnp.float32
HALF = 16


def torus(n):
    return (8, 4, 4) if n == 128 else (2, 1, n // 2)


def combine(acc, rows, ranges):
    lane = lax.broadcasted_iota(jnp.int32, (rows, ranges), 1)
    low = jnp.where(lane == 0, 0.0, pltpu.roll(acc[:rows], 1, 1))
    high = jnp.where(lane == ranges - 1, 0.0, pltpu.roll(acc[2 * rows :], ranges - 1, 1))
    return low + acc[rows : 2 * rows] + high


def column_of(row):
    k = row.shape[1]
    a = lax.broadcasted_iota(jnp.int32, (k, k), 0)
    b = lax.broadcasted_iota(jnp.int32, (k, k), 1)
    return jnp.sum(jnp.where(a == b, jnp.broadcast_to(row, (k, k)), 0.0), axis=1, keepdims=True)


def kernel(
    n,
    feat,
    w1_in,
    b1_in,
    w2_in,
    b2_in,
    req_in,
    slot_in,
    frac_in,
    wexp,
    b3_in,
    out,
    fv,
    x1,
    w1,
    b1,
    w2,
    b2,
    req,
    slot,
    frac,
    b3,
    h1,
    e1s,
    e1r,
    acc_edge,
    oha,
    ohb,
    sa,
    sb,
    keyt,
    wt,
    reqt,
    reqg,
    pbuf,
    arr,
    h2t,
    rq,
    wr,
    wx,
    rbuf,
    in_sem,
    e1_send,
    e1_recv,
    rq_send,
    rq_recv,
    rg_send,
    rg_recv,
    w_send,
    w_recv,
    g_send,
    g_recv,
    r_send,
    r_recv,
    a_send,
    a_recv,
):
    az = lax.axis_index("az")
    ch = lax.axis_index("ch")
    nz, nx, ny = torus(n)
    members = nx * ny
    groups = nz
    chans = x1.shape[0] // 4
    ranges = x1.shape[1]
    outs = w1.shape[0] // 9
    cart = slot.shape[1]
    rows = members * HALF
    hh = out.shape[0]
    share = n // 4
    right = lax.rem(az + 1, n)
    left = lax.rem(az + n - 1, n)
    my_z = az // members
    my_x = lax.rem(az, members) // ny
    my_y = lax.rem(az, ny)

    fetches = []
    pairs = (
        (feat, fv),
        (w1_in, w1),
        (req_in, req),
        (b1_in, b1),
        (w2_in, w2),
        (b2_in, b2),
        (slot_in, slot),
        (frac_in, frac),
        (b3_in, b3),
    )
    for k, (src, dst) in enumerate(pairs):
        c = pltpu.make_async_copy(src, dst, in_sem.at[k])
        c.start()
        fetches.append(c)

    side, core = ch // 2, lax.rem(ch, 2)
    peers = {
        1: side * 2 + 1 - core,
        2: (1 - side) * 2 + core,
        3: (1 - side) * 2 + 1 - core,
    }

    barrier = pltpu.get_barrier_semaphore()

    def hail(to_az, to_ch):
        pl.semaphore_signal(barrier, inc=1, device_id=(to_az, to_ch), device_id_type=MESH)

    hail(right, ch)
    hail(left, ch)
    for d in range(1, 4):
        hail(az, peers[d])

    def greet(d, _):
        to = az + d
        hail(jnp.where(to >= n, to - n, to), ch)
        return 0

    lax.fori_loop(2, n - 1, greet, 0, unroll=True)

    def at_column(col):
        return slice(col * chans, (col + 1) * chans)

    def part(w, x, col, begin, end):
        total = None
        for tap in range(3):
            src = col + tap - 1
            if begin <= src <= end:
                term = jnp.dot(
                    w[tap * 3 * outs : (tap + 1) * 3 * outs, :],
                    x[at_column(src - begin), :],
                    preferred_element_type=F32,
                )
                total = term if total is None else total + term
        return combine(total, outs, ranges)

    fetches[0].wait()
    for col in (3, 2, 0, 1):
        x1[at_column(col), :] = fv[:, col, :]
    fetches[1].wait()
    edges = ((2, 3), (3, 4), (0, -1), (1, 0))
    for k, col in edges:
        mine_only = part(w1, x1, col, 0, 3)
        acc_edge[k] = mine_only
        e1s[1 - k // 2, (k % 2) * outs : (k % 2 + 1) * outs, :] = mine_only.astype(BF)
    fetches[2].wait()

    pl.semaphore_wait(barrier, n + 2)

    def edge(src, dst, send, recv):
        copies = []
        for k, to in ((0, right), (1, left)):
            copies.append(
                pltpu.make_async_remote_copy(
                    src_ref=src.at[k],
                    dst_ref=dst.at[k],
                    send_sem=send.at[k],
                    recv_sem=recv.at[k],
                    device_id=(to, ch),
                    device_id_type=MESH,
                )
            )
        return copies

    e1 = edge(e1s, e1r, e1_send, e1_recv)
    for c in e1:
        c.start()

    ahead_z = [lax.rem(my_z + d, nz) * members for d in range(nz)]
    back_z = [lax.rem(my_z + nz - d, nz) * members for d in range(nz)]
    ahead_xy, back_xy = [], []
    for i in range(members):
        ix, iy = i // ny, i % ny
        ahead_xy.append(lax.rem(my_x + ix, nx) * ny + lax.rem(my_y + iy, ny))
        back_xy.append(lax.rem(my_x + nx - ix, nx) * ny + lax.rem(my_y + ny - iy, ny))

    def ask(k):
        p = ch * share + k
        g = p // members
        i = lax.rem(p, members) if share % members else k % members
        if share % members:
            ix, iy = i // ny, lax.rem(i, ny)
            xy = lax.rem(my_x + nx - ix, nx) * ny + lax.rem(my_y + ny - iy, ny)
        else:
            xy = back_xy[i]
        to = lax.rem(my_z + nz - lax.rem(g + i, nz), nz) * members + xy
        pltpu.make_async_remote_copy(
            src_ref=req.at[to // 4],
            dst_ref=rq.at[p],
            send_sem=rq_send,
            recv_sem=rq_recv,
            device_id=(to, ch),
            device_id_type=MESH,
        ).start()

    wcopies = []
    for d in range(1, 4):
        to = peers[d]
        c = pltpu.make_async_remote_copy(
            src_ref=wexp.at[:, pl.ds(pl.multiple_of(to * hh, hh), hh)],
            dst_ref=wr.at[ch],
            send_sem=w_send.at[d - 1],
            recv_sem=w_recv.at[d - 1],
            device_id=(az, to),
            device_id_type=MESH,
        )
        c.start()
        wcopies.append(c)
    own_w = pltpu.make_async_copy(
        wexp.at[:, pl.ds(pl.multiple_of(ch * hh, hh), hh)], wr.at[ch], in_sem.at[len(pairs)]
    )
    own_w.start()

    @pl.when(ch == 0)
    def _():
        pltpu.make_async_copy(req.at[az // 4], rq.at[0], rq_recv).start()

    @pl.when(ch != 0)
    def _():
        ask(0)

    for k in range(1, share):
        ask(k)

    fetches[3].wait()
    bias1 = column_of(b1[...])

    def mine(col):
        return pl.ds(pl.multiple_of((col + 1) * chans + ch * outs, outs), outs)

    def block_of(col, owner):
        return pl.ds(pl.multiple_of((col + 1) * chans + owner * outs, outs), outs)

    def pass_block(col, owner, to, lane):
        c = pltpu.make_async_remote_copy(
            src_ref=h1.at[block_of(col, owner)],
            dst_ref=h1.at[block_of(col, owner)],
            send_sem=g_send.at[col + 1, lane - 1],
            recv_sem=g_recv.at[col + 1, lane - 1],
            device_id=(az, peers[to]),
            device_id_type=MESH,
        )
        c.start()
        return c

    gathers = {}
    for col in (1, 2):
        h1[mine(col), :] = jnp.maximum(part(w1, x1, col, 0, 3) + bias1, 0.0).astype(BF)
        gathers[col] = [pass_block(col, ch, d, d) for d in (2, 1)]

    def asked(ref, at, count, send, recv):
        return pltpu.make_async_remote_copy(
            src_ref=ref.at[pl.ds(at, count)],
            dst_ref=ref.at[pl.ds(at, count)],
            send_sem=send,
            recv_sem=recv,
            device_id=(right, ch),
            device_id_type=MESH,
        )

    for c in e1:
        c.wait_recv()
    late = ((1, 0), (2, 3), (0, -1), (3, 4))
    for k, col in late:
        other = e1r[k // 2, (k % 2) * outs : (k % 2 + 1) * outs, :].astype(F32)
        h1[mine(col), :] = jnp.maximum(acc_edge[k] + other + bias1, 0.0).astype(BF)
        gathers[col] = [pass_block(col, ch, d, d) for d in (2, 1)]
    for col in (1, 2):
        gathers[col][0].wait_recv()
        gathers[col].append(pass_block(col, peers[2], 1, 3))

    asked(rq, 0, share, rq_send, rq_recv).wait_recv()
    passed = []
    for d in range(1, 4):
        at = pl.ds(pl.multiple_of(ch * share, share), share)
        c = pltpu.make_async_remote_copy(
            src_ref=rq.at[at],
            dst_ref=rq.at[at],
            send_sem=rg_send.at[d - 1],
            recv_sem=rg_recv.at[d - 1],
            device_id=(az, peers[d]),
            device_id_type=MESH,
        )
        c.start()
        passed.append(c)

    own_w.wait()
    for d in range(3):
        wcopies[d].wait_recv()
    for g in range(4):
        block = wr[g].astype(F32)
        zero = jnp.zeros((128 - outs, hh), F32)
        wx[0, :, g * 128 : (g + 1) * 128] = jnp.concatenate([block, zero], axis=0).T.astype(BF)
        wx[1, :, g * 128 : (g + 1) * 128] = jnp.concatenate([zero, block], axis=0).T.astype(BF)
    for k in (4, 5, 8):
        fetches[k].wait()
    bias2 = column_of(b2[...])
    bias3 = column_of(b3[...])

    for k, col in late:
        gathers[col][0].wait_recv()
        gathers[col].append(pass_block(col, peers[2], 1, 3))

    def place(col, value):
        zero = jnp.zeros((128 - outs, ranges), F32)
        at = slice(col * ranges, (col + 1) * ranges)
        h2t[0, at, :] = jnp.concatenate([value, zero], axis=0).T.astype(BF)
        h2t[1, at, :] = jnp.concatenate([zero, value], axis=0).T.astype(BF)

    def second(col):
        place(col, jnp.maximum(part(w2, h1, col, -1, 4) + bias2, 0.0))

    def arrived(col):
        gathers[col][1].wait_recv()
        gathers[col][2].wait_recv()

    arrived(1)
    arrived(2)
    arrived(0)
    second(1)
    arrived(3)
    second(2)

    for c in passed:
        c.wait_recv()
    reqt[...] = rq[:, 0, :].T
    wanted = reqt[pl.ds(pl.multiple_of(lax.rem(az, 4) * 2 * HALF, 2 * HALF), 2 * HALF), :]
    for g in range(groups):
        reqg[g] = wanted[:, g * members : (g + 1) * members]

    def one_hot(g, _):
        some = reqg[g]
        spot = lax.broadcasted_iota(jnp.int32, (HALF, 4 * ranges), 1)
        for i in range(members):
            at = pl.ds(pl.multiple_of(g * rows + i * HALF, HALF), HALF)
            oha[at, :] = jnp.where(spot == some[:HALF, i : i + 1], 1.0, 0.0).astype(BF)
            ohb[at, :] = jnp.where(spot == some[HALF:, i : i + 1], 1.0, 0.0).astype(BF)
        return 0

    lax.fori_loop(0, groups, one_hot, 0)

    arrived(-1)
    second(0)
    arrived(4)
    second(3)

    for g in range(groups):
        at = slice(g * rows, (g + 1) * rows)
        picked = jnp.dot(oha[at, :], h2t[0], preferred_element_type=F32)
        picked += jnp.dot(ohb[at, :], h2t[1], preferred_element_type=F32)
        pbuf[g] = picked.astype(BF)

        for i in range(1 if g == 0 else 0, members):
            block = slice(i * HALF, (i + 1) * HALF)
            pltpu.make_async_remote_copy(
                src_ref=pbuf.at[g, block],
                dst_ref=arr.at[g, block],
                send_sem=a_send.at[g],
                recv_sem=a_recv.at[g],
                device_id=(ahead_z[(g + i) % nz] + ahead_xy[i], ch),
                device_id_type=MESH,
            ).start()
        if g == 0:
            arr[0, :HALF, :] = pbuf[0, :HALF, :]

    fetches[6].wait()
    fetches[7].wait()
    q = slot[...]
    sector = lax.shift_right_logical(q, 5)
    low = jnp.bitwise_and(q, HALF - 1)
    upper = jnp.bitwise_and(q, HALF) != 0
    dx = jnp.bitwise_and(my_x - jnp.bitwise_and(sector // ny, nx - 1), nx - 1)
    dy = jnp.bitwise_and(my_y - jnp.bitwise_and(sector, ny - 1), ny - 1)
    place_i = dx * ny + dy
    place_g = jnp.bitwise_and(my_z - sector // members - place_i, nz - 1)
    m = (place_g * members + place_i) * HALF + low
    keys = jnp.concatenate(
        [jnp.where(upper, -1, m), jnp.where(upper, m, -1)]
        + [jnp.zeros((120, cart), jnp.int32)],
        axis=0,
    )
    keyt[...] = keys.T
    u, v = frac[0:1, :], frac[1:2, :]
    weights = jnp.concatenate(
        [(1.0 - u) * (1.0 - v), u * (1.0 - v), (1.0 - u) * v, u * v]
        + [jnp.zeros((124, cart), F32)],
        axis=0,
    )
    wt[...] = weights.T
    width = min(128, n * HALF)

    def s_rows(b, _):
        at = pl.ds(pl.multiple_of(b * 16, 16), 16)
        spot = lax.broadcasted_iota(jnp.int32, (16, width), 1).astype(jnp.int16)
        parts = [jnp.broadcast_to(wt[at, k : k + 1], (16, width)).astype(BF) for k in range(4)]
        for base, ref in ((0, sa), (4, sb)):
            found = [
                jnp.broadcast_to(keyt[at, base + k : base + k + 1], (16, width)).astype(jnp.int16)
                for k in range(4)
            ]
            for j in range(n * HALF // width):
                here = spot + jnp.int16(j * width)
                total = jnp.zeros((16, width), BF)
                for k in range(4):
                    total = jnp.where(here == found[k], parts[k], total)
                ref[at, j * width : (j + 1) * width] = total
        return 0

    lax.fori_loop(0, cart // 16, s_rows, 0, unroll=2 if cart >= 32 else 1)

    def whole(g):
        size = rows - HALF if g == 0 else rows
        return pltpu.make_async_remote_copy(
            src_ref=pbuf.at[g, pl.ds(0, size)],
            dst_ref=arr.at[g, pl.ds(0, size)],
            send_sem=a_send.at[g],
            recv_sem=a_recv.at[g],
            device_id=(right, ch),
            device_id_type=MESH,
        )

    half = cart // 2
    piece = half // 2
    sums = {}
    for g in range(groups):
        whole(g).wait_recv()
        at = slice(g * rows, (g + 1) * rows)
        for h in range(2):
            for p in range(2):
                cells = slice(p * half + h * piece, p * half + (h + 1) * piece)
                for name, ref in (("a", sa), ("b", sb)):
                    term = jnp.dot(ref[cells, at], arr[g], preferred_element_type=F32)
                    key = (h, p, name)
                    sums[key] = term if g == 0 else sums[key] + term
    lane = lax.broadcasted_iota(jnp.int32, (piece, 128), 1)
    rcopies = {}
    for h in range(2):
        first = sums[h, 0, "a"] + pltpu.roll(sums[h, 0, "b"], 64, 1)
        second = pltpu.roll(sums[h, 1, "a"], 64, 1) + sums[h, 1, "b"]
        at = slice(h * piece, (h + 1) * piece)
        rbuf[ch, at, :] = jnp.where(lane < 64, first, second).astype(BF)
        rcopies[h] = []
        for d in (3, 2, 1):
            c = pltpu.make_async_remote_copy(
                src_ref=rbuf.at[ch, at],
                dst_ref=rbuf.at[ch, at],
                send_sem=r_send.at[h, d - 1],
                recv_sem=r_recv.at[h, d - 1],
                device_id=(az, peers[d]),
                device_id_type=MESH,
            )
            c.start()
            rcopies[h].append(c)
    for h in range(2):
        for c in rcopies[h]:
            c.wait_recv()
        at = slice(h * piece, (h + 1) * piece)
        for p in range(2):
            sum_p = jnp.zeros((hh, piece), F32)
            for g in range(4):
                sum_p += lax.dot_general(
                    wx[p, :, g * 128 : (g + 1) * 128],
                    rbuf[g, at, :],
                    (((1,), (1,)), ((), ())),
                    preferred_element_type=F32,
                )
            cells = slice(p * half + h * piece, p * half + (h + 1) * piece)
            out[:, cells] = (sum_p + bias3).astype(BF)

    for c in e1 + wcopies + passed + rcopies[0] + rcopies[1] + [c for k in range(-1, 5) for c in gathers[k]]:
        c.wait_send()

    @pl.when(ch == 0)
    def _():
        asked(rq, 0, share - 1, rq_send, rq_recv).wait_send()

    @pl.when(ch != 0)
    def _():
        asked(rq, 0, share, rq_send, rq_recv).wait_send()

    for g in range(groups):
        whole(g).wait_send()


def local(
    features,
    conv1_weight,
    conv1_bias,
    conv2_weight,
    conv2_bias,
    request_cell,
    corner_slot,
    corner_frac,
    expand_weight,
    expand_bias,
):
    n = lax.axis_size("az")
    chans, columns, ranges = features.shape
    outs = conv1_weight.shape[0]
    cart = corner_slot.shape[1]
    hh = expand_bias.shape[0]
    groups = torus(n)[0]
    members = n // groups
    rows = members * HALF

    w1 = conv1_weight.transpose(1, 2, 0, 3).reshape(9 * outs, chans)
    w2 = conv2_weight.transpose(1, 2, 0, 3).reshape(9 * outs, chans)
    args = (
        features,
        w1,
        conv1_bias.reshape(1, outs),
        w2,
        conv2_bias.reshape(1, outs),
        request_cell.reshape(n * 2 * HALF // 128, 1, 128),
        corner_slot,
        corner_frac,
        expand_weight,
        expand_bias.reshape(1, hh),
    )
    dma = pltpu.SemaphoreType.DMA
    return pl.pallas_call(
        functools.partial(kernel, n),
        out_shape=jax.ShapeDtypeStruct((hh, cart), BF),
        in_specs=[pl.BlockSpec(memory_space=pl.ANY)] * len(args),
        out_specs=pl.BlockSpec(memory_space=pltpu.VMEM),
        scratch_shapes=[
            pltpu.VMEM((chans, 4, ranges), BF),
            pltpu.VMEM((4 * chans, ranges), BF),
            pltpu.VMEM((9 * outs, chans), BF),
            pltpu.VMEM((1, outs), F32),
            pltpu.VMEM((9 * outs, chans), BF),
            pltpu.VMEM((1, outs), F32),
            pltpu.VMEM((n * 2 * HALF // 128, 1, 128), jnp.int32),
            pltpu.VMEM((4, cart), jnp.int32),
            pltpu.VMEM((2, cart), F32),
            pltpu.VMEM((1, hh), F32),
            pltpu.VMEM((6 * chans, ranges), BF),
            pltpu.VMEM((2, 2 * outs, ranges), BF),
            pltpu.VMEM((2, 2 * outs, ranges), BF),
            pltpu.VMEM((4, outs, ranges), F32),
            pltpu.VMEM((n * HALF, 4 * ranges), BF),
            pltpu.VMEM((n * HALF, 4 * ranges), BF),
            pltpu.VMEM((cart, n * HALF), BF),
            pltpu.VMEM((cart, n * HALF), BF),
            pltpu.VMEM((cart, 128), jnp.int32),
            pltpu.VMEM((cart, 128), F32),
            pltpu.VMEM((128, n), jnp.int32),
            pltpu.VMEM((groups, 2 * HALF, members), jnp.int32),
            pltpu.VMEM((groups, rows, 128), BF),
            pltpu.VMEM((groups, rows, 128), BF),
            pltpu.VMEM((2, 4 * ranges, 128), BF),
            pltpu.VMEM((n, 1, 128), jnp.int32),
            pltpu.VMEM((4, outs, hh), BF),
            pltpu.VMEM((2, hh, 512), BF),
            pltpu.VMEM((4, cart // 2, 128), BF),
            dma((10,)),
            dma((2,)),
            dma((2,)),
            dma,
            dma,
            dma((3,)),
            dma((3,)),
            dma((3,)),
            dma((3,)),
            dma((6, 3)),
            dma((6, 3)),
            dma((2, 3)),
            dma((2, 3)),
            dma((groups,)),
            dma((groups,)),
        ],
        compiler_params=pltpu.CompilerParams(
            collective_id=0, has_side_effects=True, vmem_limit_bytes=48 * 1024 * 1024
        ),
        cost_estimate=pl.CostEstimate(
            flops=4 * 10**9, bytes_accessed=2 * 10**6, transcendentals=0
        ),
    )(*[pltpu.with_memory_space_constraint(x, pltpu.HBM) for x in args])


def solution(mesh):
    return jax.shard_map(
        local,
        mesh=mesh,
        in_specs=(
            P(None, "az", None),
            P("ch", None, None, None),
            P("ch"),
            P("ch", None, None, None),
            P("ch"),
            P("az"),
            P(None, "az"),
            P(None, "az"),
            P("ch", None),
            P("ch"),
        ),
        out_specs=P("ch", "az"),
        check_vma=False,
    )
```

```python
import functools

import jax
import jax.numpy as jnp
from jax import lax
from jax.experimental import pallas as pl
from jax.experimental.pallas import tpu as pltpu
from jax.sharding import PartitionSpec as P

MESH = pl.DeviceIdType.MESH
BF = jnp.bfloat16
F32 = jnp.float32
HALF = 16


def torus(n):
    return (8, 4, 4) if n == 128 else (2, 1, n // 2)


def combine(acc, rows, ranges):
    lane = lax.broadcasted_iota(jnp.int32, (rows, ranges), 1)
    low = jnp.where(lane == 0, 0.0, pltpu.roll(acc[:rows], 1, 1))
    high = jnp.where(lane == ranges - 1, 0.0, pltpu.roll(acc[2 * rows :], ranges - 1, 1))
    return low + acc[rows : 2 * rows] + high


def column_of(row):
    k = row.shape[1]
    a = lax.broadcasted_iota(jnp.int32, (k, k), 0)
    b = lax.broadcasted_iota(jnp.int32, (k, k), 1)
    return jnp.sum(jnp.where(a == b, jnp.broadcast_to(row, (k, k)), 0.0), axis=1, keepdims=True)


def kernel(
    n,
    feat,
    w1_in,
    b1_in,
    w2_in,
    b2_in,
    req_in,
    slot_in,
    frac_in,
    wexp,
    b3_in,
    out,
    fv,
    x1,
    w1,
    b1,
    w2,
    b2,
    req,
    slot,
    frac,
    b3,
    h1,
    e1s,
    e1r,
    acc_edge,
    oha,
    ohb,
    sa,
    sb,
    keyt,
    wt,
    reqt,
    reqg,
    pbuf,
    arr,
    h2t,
    rq,
    wr,
    wx,
    rbuf,
    in_sem,
    e1_send,
    e1_recv,
    rq_send,
    rq_recv,
    w_send,
    w_recv,
    g_send,
    g_recv,
    r_send,
    r_recv,
    a_send,
    a_recv,
):
    az = lax.axis_index("az")
    ch = lax.axis_index("ch")
    nz, nx, ny = torus(n)
    members = nx * ny
    groups = nz
    chans = x1.shape[0] // 4
    ranges = x1.shape[1]
    outs = w1.shape[0] // 9
    cart = slot.shape[1]
    rows = members * HALF
    hh = out.shape[0]
    right = lax.rem(az + 1, n)
    left = lax.rem(az + n - 1, n)
    my_z = az // members
    my_x = lax.rem(az, members) // ny
    my_y = lax.rem(az, ny)

    fetches = []
    pairs = (
        (feat, fv),
        (w1_in, w1),
        (req_in, req),
        (b1_in, b1),
        (w2_in, w2),
        (b2_in, b2),
        (slot_in, slot),
        (frac_in, frac),
        (b3_in, b3),
    )
    for k, (src, dst) in enumerate(pairs):
        c = pltpu.make_async_copy(src, dst, in_sem.at[k])
        c.start()
        fetches.append(c)

    side, core = ch // 2, lax.rem(ch, 2)
    peers = {
        1: side * 2 + 1 - core,
        2: (1 - side) * 2 + core,
        3: (1 - side) * 2 + 1 - core,
    }

    barrier = pltpu.get_barrier_semaphore()

    def hail(to_az, to_ch):
        pl.semaphore_signal(barrier, inc=1, device_id=(to_az, to_ch), device_id_type=MESH)

    hail(right, ch)
    hail(left, ch)
    for d in range(1, 4):
        hail(az, peers[d])

    def greet(d, _):
        to = az + d
        hail(jnp.where(to >= n, to - n, to), ch)
        return 0

    lax.fori_loop(2, n - 1, greet, 0, unroll=True)

    def at_column(col):
        return slice(col * chans, (col + 1) * chans)

    def part(w, x, col, begin, end):
        total = None
        for tap in range(3):
            src = col + tap - 1
            if begin <= src <= end:
                term = jnp.dot(
                    w[tap * 3 * outs : (tap + 1) * 3 * outs, :],
                    x[at_column(src - begin), :],
                    preferred_element_type=F32,
                )
                total = term if total is None else total + term
        return combine(total, outs, ranges)

    fetches[0].wait()
    for col in (3, 2, 0, 1):
        x1[at_column(col), :] = fv[:, col, :]
    fetches[1].wait()
    edges = ((2, 3), (3, 4), (0, -1), (1, 0))
    for k, col in edges:
        mine_only = part(w1, x1, col, 0, 3)
        acc_edge[k] = mine_only
        e1s[1 - k // 2, (k % 2) * outs : (k % 2 + 1) * outs, :] = mine_only.astype(BF)
    fetches[2].wait()

    pl.semaphore_wait(barrier, n + 2)

    def edge(src, dst, send, recv):
        copies = []
        for k, to in ((0, right), (1, left)):
            copies.append(
                pltpu.make_async_remote_copy(
                    src_ref=src.at[k],
                    dst_ref=dst.at[k],
                    send_sem=send.at[k],
                    recv_sem=recv.at[k],
                    device_id=(to, ch),
                    device_id_type=MESH,
                )
            )
        return copies

    e1 = edge(e1s, e1r, e1_send, e1_recv)
    for c in e1:
        c.start()

    ahead_z = [lax.rem(my_z + d, nz) * members for d in range(nz)]
    back_z = [lax.rem(my_z + nz - d, nz) * members for d in range(nz)]
    ahead_xy, back_xy = [], []
    for i in range(members):
        ix, iy = i // ny, i % ny
        ahead_xy.append(lax.rem(my_x + ix, nx) * ny + lax.rem(my_y + iy, ny))
        back_xy.append(lax.rem(my_x + nx - ix, nx) * ny + lax.rem(my_y + ny - iy, ny))

    def ask(g, i):
        to = lax.rem(my_z + nz - lax.rem(g + i, nz), nz) * members + back_xy[i]
        pltpu.make_async_remote_copy(
            src_ref=req.at[to // 4],
            dst_ref=rq.at[g * members + i],
            send_sem=rq_send,
            recv_sem=rq_recv,
            device_id=(to, ch),
            device_id_type=MESH,
        ).start()

    def ask_first(g, _):
        ask(g, 0)
        return 0

    def ask_rest(g, _):
        for i in range(1, members):
            ask(g, i)
        return 0

    wcopies = []
    for d in range(1, 4):
        to = peers[d]
        c = pltpu.make_async_remote_copy(
            src_ref=wexp.at[:, pl.ds(pl.multiple_of(to * hh, hh), hh)],
            dst_ref=wr.at[ch],
            send_sem=w_send.at[d - 1],
            recv_sem=w_recv.at[d - 1],
            device_id=(az, to),
            device_id_type=MESH,
        )
        c.start()
        wcopies.append(c)
    own_w = pltpu.make_async_copy(
        wexp.at[:, pl.ds(pl.multiple_of(ch * hh, hh), hh)], wr.at[ch], in_sem.at[len(pairs)]
    )
    own_w.start()

    lax.fori_loop(1, groups, ask_first, 0)
    lax.fori_loop(0, groups, ask_rest, 0)
    rq[0] = req[az // 4]

    fetches[3].wait()
    bias1 = column_of(b1[...])

    def mine(col):
        return pl.ds(pl.multiple_of((col + 1) * chans + ch * outs, outs), outs)

    def block_of(col, owner):
        return pl.ds(pl.multiple_of((col + 1) * chans + owner * outs, outs), outs)

    def pass_block(col, owner, to, lane):
        c = pltpu.make_async_remote_copy(
            src_ref=h1.at[block_of(col, owner)],
            dst_ref=h1.at[block_of(col, owner)],
            send_sem=g_send.at[col + 1, lane - 1],
            recv_sem=g_recv.at[col + 1, lane - 1],
            device_id=(az, peers[to]),
            device_id_type=MESH,
        )
        c.start()
        return c

    gathers = {}
    for col in (1, 2):
        h1[mine(col), :] = jnp.maximum(part(w1, x1, col, 0, 3) + bias1, 0.0).astype(BF)
        gathers[col] = [pass_block(col, ch, d, d) for d in (2, 1)]

    def asked():
        return pltpu.make_async_remote_copy(
            src_ref=rq.at[pl.ds(1, n - 1)],
            dst_ref=rq.at[pl.ds(1, n - 1)],
            send_sem=rq_send,
            recv_sem=rq_recv,
            device_id=(right, ch),
            device_id_type=MESH,
        )

    for c in e1:
        c.wait_recv()
    late = ((1, 0), (2, 3), (0, -1), (3, 4))
    for k, col in late:
        other = e1r[k // 2, (k % 2) * outs : (k % 2 + 1) * outs, :].astype(F32)
        h1[mine(col), :] = jnp.maximum(acc_edge[k] + other + bias1, 0.0).astype(BF)
        gathers[col] = [pass_block(col, ch, d, d) for d in (2, 1)]
    for col in (1, 2):
        gathers[col][0].wait_recv()
        gathers[col].append(pass_block(col, peers[2], 1, 3))

    def hand_on(col):
        gathers[col][0].wait_recv()
        gathers[col].append(pass_block(col, peers[2], 1, 3))

    asked().wait_recv()
    reqt[...] = rq[:, 0, :].T
    wanted = reqt[pl.ds(pl.multiple_of(lax.rem(az, 4) * 2 * HALF, 2 * HALF), 2 * HALF), :]
    for g in range(groups):
        reqg[g] = wanted[:, g * members : (g + 1) * members]

    def one_hot(g, _):
        some = reqg[g]
        spot = lax.broadcasted_iota(jnp.int32, (HALF, 4 * ranges), 1)
        for i in range(members):
            at = pl.ds(pl.multiple_of(g * rows + i * HALF, HALF), HALF)
            oha[at, :] = jnp.where(spot == some[:HALF, i : i + 1], 1.0, 0.0).astype(BF)
            ohb[at, :] = jnp.where(spot == some[HALF:, i : i + 1], 1.0, 0.0).astype(BF)
        return 0

    lax.fori_loop(0, groups, one_hot, 0)

    hand_on(0)
    hand_on(3)

    own_w.wait()
    for d in range(3):
        wcopies[d].wait_recv()
    for g in range(4):
        block = wr[g].astype(F32)
        zero = jnp.zeros((128 - outs, hh), F32)
        wx[0, :, g * 128 : (g + 1) * 128] = jnp.concatenate([block, zero], axis=0).T.astype(BF)
        wx[1, :, g * 128 : (g + 1) * 128] = jnp.concatenate([zero, block], axis=0).T.astype(BF)
    for k in (4, 5, 8):
        fetches[k].wait()
    bias2 = column_of(b2[...])
    bias3 = column_of(b3[...])

    hand_on(-1)
    hand_on(4)

    def place(col, value):
        zero = jnp.zeros((128 - outs, ranges), F32)
        at = slice(col * ranges, (col + 1) * ranges)
        h2t[0, at, :] = jnp.concatenate([value, zero], axis=0).T.astype(BF)
        h2t[1, at, :] = jnp.concatenate([zero, value], axis=0).T.astype(BF)

    def second(col):
        place(col, jnp.maximum(part(w2, h1, col, -1, 4) + bias2, 0.0))

    def arrived(col):
        gathers[col][1].wait_recv()
        gathers[col][2].wait_recv()

    arrived(1)
    arrived(2)
    arrived(0)
    second(1)
    arrived(3)
    second(2)

    arrived(-1)
    second(0)
    arrived(4)
    second(3)

    for g in range(groups):
        at = slice(g * rows, (g + 1) * rows)
        picked = jnp.dot(oha[at, :], h2t[0], preferred_element_type=F32)
        picked += jnp.dot(ohb[at, :], h2t[1], preferred_element_type=F32)
        pbuf[g] = picked.astype(BF)

        for i in range(1 if g == 0 else 0, members):
            block = slice(i * HALF, (i + 1) * HALF)
            pltpu.make_async_remote_copy(
                src_ref=pbuf.at[g, block],
                dst_ref=arr.at[g, block],
                send_sem=a_send.at[g],
                recv_sem=a_recv.at[g],
                device_id=(ahead_z[(g + i) % nz] + ahead_xy[i], ch),
                device_id_type=MESH,
            ).start()
        if g == 0:
            arr[0, :HALF, :] = pbuf[0, :HALF, :]

    fetches[6].wait()
    fetches[7].wait()
    q = slot[...]
    sector = lax.shift_right_logical(q, 5)
    low = jnp.bitwise_and(q, HALF - 1)
    upper = jnp.bitwise_and(q, HALF) != 0
    dx = jnp.bitwise_and(my_x - jnp.bitwise_and(sector // ny, nx - 1), nx - 1)
    dy = jnp.bitwise_and(my_y - jnp.bitwise_and(sector, ny - 1), ny - 1)
    place_i = dx * ny + dy
    place_g = jnp.bitwise_and(my_z - sector // members - place_i, nz - 1)
    m = (place_g * members + place_i) * HALF + low
    keys = jnp.concatenate(
        [jnp.where(upper, -1, m), jnp.where(upper, m, -1)]
        + [jnp.zeros((120, cart), jnp.int32)],
        axis=0,
    )
    keyt[...] = keys.T
    u, v = frac[0:1, :], frac[1:2, :]
    weights = jnp.concatenate(
        [(1.0 - u) * (1.0 - v), u * (1.0 - v), (1.0 - u) * v, u * v]
        + [jnp.zeros((124, cart), F32)],
        axis=0,
    )
    wt[...] = weights.T
    width = min(128, n * HALF)

    def s_rows(b, _):
        at = pl.ds(pl.multiple_of(b * 16, 16), 16)
        spot = lax.broadcasted_iota(jnp.int32, (16, width), 1).astype(jnp.int16)
        parts = [jnp.broadcast_to(wt[at, k : k + 1], (16, width)).astype(BF) for k in range(4)]
        for base, ref in ((0, sa), (4, sb)):
            found = [
                jnp.broadcast_to(keyt[at, base + k : base + k + 1], (16, width)).astype(jnp.int16)
                for k in range(4)
            ]
            for j in range(n * HALF // width):
                here = spot + jnp.int16(j * width)
                total = jnp.zeros((16, width), BF)
                for k in range(4):
                    total = jnp.where(here == found[k], parts[k], total)
                ref[at, j * width : (j + 1) * width] = total
        return 0

    lax.fori_loop(0, cart // 16, s_rows, 0, unroll=2 if cart >= 32 else 1)

    def whole(g):
        size = rows - HALF if g == 0 else rows
        return pltpu.make_async_remote_copy(
            src_ref=pbuf.at[g, pl.ds(0, size)],
            dst_ref=arr.at[g, pl.ds(0, size)],
            send_sem=a_send.at[g],
            recv_sem=a_recv.at[g],
            device_id=(right, ch),
            device_id_type=MESH,
        )

    half = cart // 2
    piece = half // 2
    sums = {}
    for g in range(groups):
        whole(g).wait_recv()
        at = slice(g * rows, (g + 1) * rows)
        for h in range(2):
            for p in range(2):
                cells = slice(p * half + h * piece, p * half + (h + 1) * piece)
                for name, ref in (("a", sa), ("b", sb)):
                    term = jnp.dot(ref[cells, at], arr[g], preferred_element_type=F32)
                    key = (h, p, name)
                    sums[key] = term if g == 0 else sums[key] + term
    lane = lax.broadcasted_iota(jnp.int32, (piece, 128), 1)
    rcopies = {}
    for h in range(2):
        first = sums[h, 0, "a"] + pltpu.roll(sums[h, 0, "b"], 64, 1)
        second = pltpu.roll(sums[h, 1, "a"], 64, 1) + sums[h, 1, "b"]
        at = slice(h * piece, (h + 1) * piece)
        rbuf[ch, at, :] = jnp.where(lane < 64, first, second).astype(BF)
        rcopies[h] = []
        for d in (3, 2, 1):
            c = pltpu.make_async_remote_copy(
                src_ref=rbuf.at[ch, at],
                dst_ref=rbuf.at[ch, at],
                send_sem=r_send.at[h, d - 1],
                recv_sem=r_recv.at[h, d - 1],
                device_id=(az, peers[d]),
                device_id_type=MESH,
            )
            c.start()
            rcopies[h].append(c)
    for h in range(2):
        for c in rcopies[h]:
            c.wait_recv()
        at = slice(h * piece, (h + 1) * piece)
        for p in range(2):
            sum_p = jnp.zeros((hh, piece), F32)
            for g in range(4):
                sum_p += lax.dot_general(
                    wx[p, :, g * 128 : (g + 1) * 128],
                    rbuf[g, at, :],
                    (((1,), (1,)), ((), ())),
                    preferred_element_type=F32,
                )
            cells = slice(p * half + h * piece, p * half + (h + 1) * piece)
            out[:, cells] = (sum_p + bias3).astype(BF)

    for c in e1 + wcopies + rcopies[0] + rcopies[1] + [c for k in range(-1, 5) for c in gathers[k]]:
        c.wait_send()

    asked().wait_send()
    for g in range(groups):
        whole(g).wait_send()


def local(
    features,
    conv1_weight,
    conv1_bias,
    conv2_weight,
    conv2_bias,
    request_cell,
    corner_slot,
    corner_frac,
    expand_weight,
    expand_bias,
):
    n = lax.axis_size("az")
    chans, columns, ranges = features.shape
    outs = conv1_weight.shape[0]
    cart = corner_slot.shape[1]
    hh = expand_bias.shape[0]
    groups = torus(n)[0]
    members = n // groups
    rows = members * HALF

    w1 = conv1_weight.transpose(1, 2, 0, 3).reshape(9 * outs, chans)
    w2 = conv2_weight.transpose(1, 2, 0, 3).reshape(9 * outs, chans)
    args = (
        features,
        w1,
        conv1_bias.reshape(1, outs),
        w2,
        conv2_bias.reshape(1, outs),
        request_cell.reshape(n * 2 * HALF // 128, 1, 128),
        corner_slot,
        corner_frac,
        expand_weight,
        expand_bias.reshape(1, hh),
    )
    dma = pltpu.SemaphoreType.DMA
    return pl.pallas_call(
        functools.partial(kernel, n),
        out_shape=jax.ShapeDtypeStruct((hh, cart), BF),
        in_specs=[pl.BlockSpec(memory_space=pl.ANY)] * len(args),
        out_specs=pl.BlockSpec(memory_space=pltpu.VMEM),
        scratch_shapes=[
            pltpu.VMEM((chans, 4, ranges), BF),
            pltpu.VMEM((4 * chans, ranges), BF),
            pltpu.VMEM((9 * outs, chans), BF),
            pltpu.VMEM((1, outs), F32),
            pltpu.VMEM((9 * outs, chans), BF),
            pltpu.VMEM((1, outs), F32),
            pltpu.VMEM((n * 2 * HALF // 128, 1, 128), jnp.int32),
            pltpu.VMEM((4, cart), jnp.int32),
            pltpu.VMEM((2, cart), F32),
            pltpu.VMEM((1, hh), F32),
            pltpu.VMEM((6 * chans, ranges), BF),
            pltpu.VMEM((2, 2 * outs, ranges), BF),
            pltpu.VMEM((2, 2 * outs, ranges), BF),
            pltpu.VMEM((4, outs, ranges), F32),
            pltpu.VMEM((n * HALF, 4 * ranges), BF),
            pltpu.VMEM((n * HALF, 4 * ranges), BF),
            pltpu.VMEM((cart, n * HALF), BF),
            pltpu.VMEM((cart, n * HALF), BF),
            pltpu.VMEM((cart, 128), jnp.int32),
            pltpu.VMEM((cart, 128), F32),
            pltpu.VMEM((128, n), jnp.int32),
            pltpu.VMEM((groups, 2 * HALF, members), jnp.int32),
            pltpu.VMEM((groups, rows, 128), BF),
            pltpu.VMEM((groups, rows, 128), BF),
            pltpu.VMEM((2, 4 * ranges, 128), BF),
            pltpu.VMEM((n, 1, 128), jnp.int32),
            pltpu.VMEM((4, outs, hh), BF),
            pltpu.VMEM((2, hh, 512), BF),
            pltpu.VMEM((4, cart // 2, 128), BF),
            dma((10,)),
            dma((2,)),
            dma((2,)),
            dma,
            dma,
            dma((3,)),
            dma((3,)),
            dma((6, 3)),
            dma((6, 3)),
            dma((2, 3)),
            dma((2, 3)),
            dma((groups,)),
            dma((groups,)),
        ],
        compiler_params=pltpu.CompilerParams(
            collective_id=0, has_side_effects=True, vmem_limit_bytes=48 * 1024 * 1024
        ),
        cost_estimate=pl.CostEstimate(
            flops=4 * 10**9, bytes_accessed=2 * 10**6, transcendentals=0
        ),
    )(*[pltpu.with_memory_space_constraint(x, pltpu.HBM) for x in args])


def solution(mesh):
    return jax.shard_map(
        local,
        mesh=mesh,
        in_specs=(
            P(None, "az", None),
            P("ch", None, None, None),
            P("ch"),
            P("ch", None, None, None),
            P("ch"),
            P("az"),
            P(None, "az"),
            P(None, "az"),
            P("ch", None),
            P("ch"),
        ),
        out_specs=P("ch", "az"),
        check_vma=False,
    )
```

```python
import functools

import jax
import jax.numpy as jnp
from jax import lax
from jax.experimental import pallas as pl
from jax.experimental.pallas import tpu as pltpu
from jax.sharding import PartitionSpec as P

MESH = pl.DeviceIdType.MESH
BF = jnp.bfloat16
F32 = jnp.float32
HALF = 16


def torus(n):
    return (8, 4, 4) if n == 128 else (2, 1, n // 2)


def combine(acc, rows, ranges):
    lane = lax.broadcasted_iota(jnp.int32, (rows, ranges), 1)
    low = jnp.where(lane == 0, 0.0, pltpu.roll(acc[:rows], 1, 1))
    high = jnp.where(lane == ranges - 1, 0.0, pltpu.roll(acc[2 * rows :], ranges - 1, 1))
    return low + acc[rows : 2 * rows] + high


def column_of(row):
    k = row.shape[1]
    a = lax.broadcasted_iota(jnp.int32, (k, k), 0)
    b = lax.broadcasted_iota(jnp.int32, (k, k), 1)
    return jnp.sum(jnp.where(a == b, jnp.broadcast_to(row, (k, k)), 0.0), axis=1, keepdims=True)


def kernel(
    n,
    feat,
    w1_in,
    b1_in,
    w2_in,
    b2_in,
    req_in,
    slot_in,
    frac_in,
    wexp,
    b3_in,
    out,
    fv,
    x1,
    w1,
    b1,
    w2,
    b2,
    req,
    slot,
    frac,
    b3,
    h1,
    e1s,
    e1r,
    e2s,
    e2r,
    acc_edge,
    oha,
    ohb,
    sa,
    sb,
    keyt,
    wt,
    reqt,
    reqg,
    pbuf,
    arr,
    h2t,
    rq,
    wr,
    wx,
    rbuf,
    in_sem,
    e1_send,
    e1_recv,
    e2_send,
    e2_recv,
    rq_send,
    rq_recv,
    rg_send,
    rg_recv,
    w_send,
    w_recv,
    g_send,
    g_recv,
    r_send,
    r_recv,
    a_send,
    a_recv,
):
    az = lax.axis_index("az")
    ch = lax.axis_index("ch")
    nz, nx, ny = torus(n)
    members = nx * ny
    groups = nz
    chans = x1.shape[0] // 4
    ranges = x1.shape[1]
    outs = w1.shape[0] // 9
    cart = slot.shape[1]
    rows = members * HALF
    hh = out.shape[0]
    share = n // 4
    right = lax.rem(az + 1, n)
    left = lax.rem(az + n - 1, n)
    my_z = az // members
    my_x = lax.rem(az, members) // ny
    my_y = lax.rem(az, ny)

    fetches = []
    pairs = (
        (feat, fv),
        (w1_in, w1),
        (req_in, req),
        (b1_in, b1),
        (w2_in, w2),
        (b2_in, b2),
        (slot_in, slot),
        (frac_in, frac),
        (b3_in, b3),
    )
    for k, (src, dst) in enumerate(pairs):
        c = pltpu.make_async_copy(src, dst, in_sem.at[k])
        c.start()
        fetches.append(c)

    side, core = ch // 2, lax.rem(ch, 2)
    peers = {
        1: side * 2 + 1 - core,
        2: (1 - side) * 2 + core,
        3: (1 - side) * 2 + 1 - core,
    }

    barrier = pltpu.get_barrier_semaphore()

    def hail(to_az, to_ch):
        pl.semaphore_signal(barrier, inc=1, device_id=(to_az, to_ch), device_id_type=MESH)

    hail(right, ch)
    hail(left, ch)
    for d in range(1, 4):
        hail(az, peers[d])

    def greet(d, _):
        to = az + d
        hail(jnp.where(to >= n, to - n, to), ch)
        return 0

    lax.fori_loop(2, n - 1, greet, 0, unroll=True)

    def at_column(col):
        return slice(col * chans, (col + 1) * chans)

    def part(w, x, col):
        total = None
        for tap in range(3):
            src = col + tap - 1
            if 0 <= src <= 3:
                term = jnp.dot(
                    w[tap * 3 * outs : (tap + 1) * 3 * outs, :],
                    x[at_column(src), :],
                    preferred_element_type=F32,
                )
                total = term if total is None else total + term
        return combine(total, outs, ranges)

    fetches[0].wait()
    for col in (3, 0):
        x1[at_column(col), :] = fv[:, col, :]
    fetches[1].wait()
    e1s[0] = part(w1, x1, 4).astype(BF)
    e1s[1] = part(w1, x1, -1).astype(BF)
    fetches[2].wait()

    pl.semaphore_wait(barrier, n + 2)

    def edge(src, dst, send, recv):
        copies = []
        for k, to in ((0, right), (1, left)):
            copies.append(
                pltpu.make_async_remote_copy(
                    src_ref=src.at[k],
                    dst_ref=dst.at[k],
                    send_sem=send.at[k],
                    recv_sem=recv.at[k],
                    device_id=(to, ch),
                    device_id_type=MESH,
                )
            )
        return copies

    e1 = edge(e1s, e1r, e1_send, e1_recv)
    for c in e1:
        c.start()

    ahead_z = [lax.rem(my_z + d, nz) * members for d in range(nz)]
    back_z = [lax.rem(my_z + nz - d, nz) * members for d in range(nz)]
    ahead_xy, back_xy = [], []
    for i in range(members):
        ix, iy = i // ny, i % ny
        ahead_xy.append(lax.rem(my_x + ix, nx) * ny + lax.rem(my_y + iy, ny))
        back_xy.append(lax.rem(my_x + nx - ix, nx) * ny + lax.rem(my_y + ny - iy, ny))

    def ask(k):
        p = ch * share + k
        g = p // members
        i = lax.rem(p, members) if share % members else k % members
        if share % members:
            ix, iy = i // ny, lax.rem(i, ny)
            xy = lax.rem(my_x + nx - ix, nx) * ny + lax.rem(my_y + ny - iy, ny)
        else:
            xy = back_xy[i]
        to = lax.rem(my_z + nz - lax.rem(g + i, nz), nz) * members + xy
        pltpu.make_async_remote_copy(
            src_ref=req.at[to // 4],
            dst_ref=rq.at[p],
            send_sem=rq_send,
            recv_sem=rq_recv,
            device_id=(to, ch),
            device_id_type=MESH,
        ).start()

    wcopies = []
    for d in range(1, 4):
        to = peers[d]
        c = pltpu.make_async_remote_copy(
            src_ref=wexp.at[:, pl.ds(pl.multiple_of(to * hh, hh), hh)],
            dst_ref=wr.at[ch],
            send_sem=w_send.at[d - 1],
            recv_sem=w_recv.at[d - 1],
            device_id=(az, to),
            device_id_type=MESH,
        )
        c.start()
        wcopies.append(c)
    own_w = pltpu.make_async_copy(
        wexp.at[:, pl.ds(pl.multiple_of(ch * hh, hh), hh)], wr.at[ch], in_sem.at[len(pairs)]
    )
    own_w.start()

    @pl.when(ch == 0)
    def _():
        pltpu.make_async_copy(req.at[az // 4], rq.at[0], rq_recv).start()

    @pl.when(ch != 0)
    def _():
        ask(0)

    for k in range(1, share):
        ask(k)

    for col in (1, 2):
        x1[at_column(col), :] = fv[:, col, :]
    fetches[3].wait()
    bias1 = column_of(b1[...])

    def mine(col):
        return pl.ds(pl.multiple_of(col * chans + ch * outs, outs), outs)

    def block_of(col, owner):
        return pl.ds(pl.multiple_of(col * chans + owner * outs, outs), outs)

    def pass_block(col, owner, to, lane):
        c = pltpu.make_async_remote_copy(
            src_ref=h1.at[block_of(col, owner)],
            dst_ref=h1.at[block_of(col, owner)],
            send_sem=g_send.at[col, lane - 1],
            recv_sem=g_recv.at[col, lane - 1],
            device_id=(az, peers[to]),
            device_id_type=MESH,
        )
        c.start()
        return c

    gathers = {}
    for col in (1, 2):
        h1[mine(col), :] = jnp.maximum(part(w1, x1, col) + bias1, 0.0).astype(BF)
        gathers[col] = [pass_block(col, ch, d, d) for d in (3, 2, 1)]
    for k, col in ((1, 3), (0, 0)):
        acc_edge[k] = part(w1, x1, col) + bias1

    def asked(ref, at, count, send, recv):
        return pltpu.make_async_remote_copy(
            src_ref=ref.at[pl.ds(at, count)],
            dst_ref=ref.at[pl.ds(at, count)],
            send_sem=send,
            recv_sem=recv,
            device_id=(right, ch),
            device_id_type=MESH,
        )

    for k, col in ((1, 3), (0, 0)):
        e1[k].wait_recv()
        h1[mine(col), :] = jnp.maximum(acc_edge[k] + e1r[k].astype(F32), 0.0).astype(BF)
        gathers[col] = [pass_block(col, ch, d, d) for d in (3, 2, 1)]
    own_w.wait()
    for d in range(3):
        wcopies[d].wait_recv()
    for g in range(4):
        block = wr[g].astype(F32)
        zero = jnp.zeros((128 - outs, hh), F32)
        wx[0, :, g * 128 : (g + 1) * 128] = jnp.concatenate([block, zero], axis=0).T.astype(BF)
        wx[1, :, g * 128 : (g + 1) * 128] = jnp.concatenate([zero, block], axis=0).T.astype(BF)
    for k in (4, 5, 8):
        fetches[k].wait()
    bias2 = column_of(b2[...])
    bias3 = column_of(b3[...])

    asked(rq, 0, share, rq_send, rq_recv).wait_recv()
    passed = []
    for d in range(1, 4):
        at = pl.ds(pl.multiple_of(ch * share, share), share)
        c = pltpu.make_async_remote_copy(
            src_ref=rq.at[at],
            dst_ref=rq.at[at],
            send_sem=rg_send.at[d - 1],
            recv_sem=rg_recv.at[d - 1],
            device_id=(az, peers[d]),
            device_id_type=MESH,
        )
        c.start()
        passed.append(c)

    e2 = edge(e2s, e2r, e2_send, e2_recv)
    for k, col, to in ((0, 3, 4), (1, 0, -1)):
        for c in gathers[col]:
            c.wait_recv()
        e2s[k] = part(w2, h1, to).astype(BF)
        e2[k].start()
    for col in (1, 2):
        for c in gathers[col]:
            c.wait_recv()

    def place(col, value):
        zero = jnp.zeros((128 - outs, ranges), F32)
        at = slice(col * ranges, (col + 1) * ranges)
        h2t[0, at, :] = jnp.concatenate([value, zero], axis=0).T.astype(BF)
        h2t[1, at, :] = jnp.concatenate([zero, value], axis=0).T.astype(BF)

    for col in (1, 2):
        place(col, jnp.maximum(part(w2, h1, col) + bias2, 0.0))
    for k, col in ((0, 0), (1, 3)):
        acc_edge[k] = part(w2, h1, col) + bias2

    for c in passed:
        c.wait_recv()
    reqt[...] = rq[:, 0, :].T
    wanted = reqt[pl.ds(pl.multiple_of(lax.rem(az, 4) * 2 * HALF, 2 * HALF), 2 * HALF), :]
    for g in range(groups):
        reqg[g] = wanted[:, g * members : (g + 1) * members]

    def one_hot(g, _):
        some = reqg[g]
        spot = lax.broadcasted_iota(jnp.int32, (HALF, 4 * ranges), 1)
        for i in range(members):
            at = pl.ds(pl.multiple_of(g * rows + i * HALF, HALF), HALF)
            oha[at, :] = jnp.where(spot == some[:HALF, i : i + 1], 1.0, 0.0).astype(BF)
            ohb[at, :] = jnp.where(spot == some[HALF:, i : i + 1], 1.0, 0.0).astype(BF)
        return 0

    lax.fori_loop(0, groups, one_hot, 0)

    for k, col in ((0, 0), (1, 3)):
        e2[k].wait_recv()
        place(col, jnp.maximum(acc_edge[k] + e2r[k].astype(F32), 0.0))

    for g in range(groups):
        at = slice(g * rows, (g + 1) * rows)
        picked = jnp.dot(oha[at, :], h2t[0], preferred_element_type=F32)
        picked += jnp.dot(ohb[at, :], h2t[1], preferred_element_type=F32)
        pbuf[g] = picked.astype(BF)

        for i in range(1 if g == 0 else 0, members):
            block = slice(i * HALF, (i + 1) * HALF)
            pltpu.make_async_remote_copy(
                src_ref=pbuf.at[g, block],
                dst_ref=arr.at[g, block],
                send_sem=a_send.at[g],
                recv_sem=a_recv.at[g],
                device_id=(ahead_z[(g + i) % nz] + ahead_xy[i], ch),
                device_id_type=MESH,
            ).start()
        if g == 0:
            arr[0, :HALF, :] = pbuf[0, :HALF, :]

    fetches[6].wait()
    fetches[7].wait()
    q = slot[...]
    sector = lax.shift_right_logical(q, 5)
    low = jnp.bitwise_and(q, HALF - 1)
    upper = jnp.bitwise_and(q, HALF) != 0
    dx = jnp.bitwise_and(my_x - jnp.bitwise_and(sector // ny, nx - 1), nx - 1)
    dy = jnp.bitwise_and(my_y - jnp.bitwise_and(sector, ny - 1), ny - 1)
    place_i = dx * ny + dy
    place_g = jnp.bitwise_and(my_z - sector // members - place_i, nz - 1)
    m = (place_g * members + place_i) * HALF + low
    keys = jnp.concatenate(
        [jnp.where(upper, -1, m), jnp.where(upper, m, -1)]
        + [jnp.zeros((120, cart), jnp.int32)],
        axis=0,
    )
    keyt[...] = keys.T
    u, v = frac[0:1, :], frac[1:2, :]
    weights = jnp.concatenate(
        [(1.0 - u) * (1.0 - v), u * (1.0 - v), (1.0 - u) * v, u * v]
        + [jnp.zeros((124, cart), F32)],
        axis=0,
    )
    wt[...] = weights.T
    width = min(128, n * HALF)

    def s_rows(b, _):
        at = pl.ds(pl.multiple_of(b * 16, 16), 16)
        spot = lax.broadcasted_iota(jnp.int32, (16, width), 1).astype(jnp.int16)
        parts = [jnp.broadcast_to(wt[at, k : k + 1], (16, width)).astype(BF) for k in range(4)]
        for base, ref in ((0, sa), (4, sb)):
            found = [
                jnp.broadcast_to(keyt[at, base + k : base + k + 1], (16, width)).astype(jnp.int16)
                for k in range(4)
            ]
            for j in range(n * HALF // width):
                here = spot + jnp.int16(j * width)
                total = jnp.zeros((16, width), BF)
                for k in range(4):
                    total = jnp.where(here == found[k], parts[k], total)
                ref[at, j * width : (j + 1) * width] = total
        return 0

    lax.fori_loop(0, cart // 16, s_rows, 0, unroll=2 if cart >= 32 else 1)

    def whole(g):
        size = rows - HALF if g == 0 else rows
        return pltpu.make_async_remote_copy(
            src_ref=pbuf.at[g, pl.ds(0, size)],
            dst_ref=arr.at[g, pl.ds(0, size)],
            send_sem=a_send.at[g],
            recv_sem=a_recv.at[g],
            device_id=(right, ch),
            device_id_type=MESH,
        )

    half = cart // 2
    piece = half // 2
    sums = {}
    for g in range(groups):
        whole(g).wait_recv()
        at = slice(g * rows, (g + 1) * rows)
        for h in range(2):
            for p in range(2):
                cells = slice(p * half + h * piece, p * half + (h + 1) * piece)
                for name, ref in (("a", sa), ("b", sb)):
                    term = jnp.dot(ref[cells, at], arr[g], preferred_element_type=F32)
                    key = (h, p, name)
                    sums[key] = term if g == 0 else sums[key] + term
    lane = lax.broadcasted_iota(jnp.int32, (piece, 128), 1)
    rcopies = {}
    for h in range(2):
        first = sums[h, 0, "a"] + pltpu.roll(sums[h, 0, "b"], 64, 1)
        second = pltpu.roll(sums[h, 1, "a"], 64, 1) + sums[h, 1, "b"]
        at = slice(h * piece, (h + 1) * piece)
        rbuf[ch, at, :] = jnp.where(lane < 64, first, second).astype(BF)
        rcopies[h] = []
        for d in (3, 2, 1):
            c = pltpu.make_async_remote_copy(
                src_ref=rbuf.at[ch, at],
                dst_ref=rbuf.at[ch, at],
                send_sem=r_send.at[h, d - 1],
                recv_sem=r_recv.at[h, d - 1],
                device_id=(az, peers[d]),
                device_id_type=MESH,
            )
            c.start()
            rcopies[h].append(c)
    for h in range(2):
        for c in rcopies[h]:
            c.wait_recv()
        at = slice(h * piece, (h + 1) * piece)
        for p in range(2):
            sum_p = jnp.zeros((hh, piece), F32)
            for g in range(4):
                sum_p += lax.dot_general(
                    wx[p, :, g * 128 : (g + 1) * 128],
                    rbuf[g, at, :],
                    (((1,), (1,)), ((), ())),
                    preferred_element_type=F32,
                )
            cells = slice(p * half + h * piece, p * half + (h + 1) * piece)
            out[:, cells] = (sum_p + bias3).astype(BF)

    for c in e1 + e2 + wcopies + passed + rcopies[0] + rcopies[1] + [c for k in range(4) for c in gathers[k]]:
        c.wait_send()

    @pl.when(ch == 0)
    def _():
        asked(rq, 0, share - 1, rq_send, rq_recv).wait_send()

    @pl.when(ch != 0)
    def _():
        asked(rq, 0, share, rq_send, rq_recv).wait_send()

    for g in range(groups):
        whole(g).wait_send()


def local(
    features,
    conv1_weight,
    conv1_bias,
    conv2_weight,
    conv2_bias,
    request_cell,
    corner_slot,
    corner_frac,
    expand_weight,
    expand_bias,
):
    n = lax.axis_size("az")
    chans, columns, ranges = features.shape
    outs = conv1_weight.shape[0]
    cart = corner_slot.shape[1]
    hh = expand_bias.shape[0]
    groups = torus(n)[0]
    members = n // groups
    rows = members * HALF

    w1 = conv1_weight.transpose(1, 2, 0, 3).reshape(9 * outs, chans)
    w2 = conv2_weight.transpose(1, 2, 0, 3).reshape(9 * outs, chans)
    args = (
        features,
        w1,
        conv1_bias.reshape(1, outs),
        w2,
        conv2_bias.reshape(1, outs),
        request_cell.reshape(n * 2 * HALF // 128, 1, 128),
        corner_slot,
        corner_frac,
        expand_weight,
        expand_bias.reshape(1, hh),
    )
    dma = pltpu.SemaphoreType.DMA
    return pl.pallas_call(
        functools.partial(kernel, n),
        out_shape=jax.ShapeDtypeStruct((hh, cart), BF),
        in_specs=[pl.BlockSpec(memory_space=pl.ANY)] * len(args),
        out_specs=pl.BlockSpec(memory_space=pltpu.VMEM),
        scratch_shapes=[
            pltpu.VMEM((chans, 4, ranges), BF),
            pltpu.VMEM((4 * chans, ranges), BF),
            pltpu.VMEM((9 * outs, chans), BF),
            pltpu.VMEM((1, outs), F32),
            pltpu.VMEM((9 * outs, chans), BF),
            pltpu.VMEM((1, outs), F32),
            pltpu.VMEM((n * 2 * HALF // 128, 1, 128), jnp.int32),
            pltpu.VMEM((4, cart), jnp.int32),
            pltpu.VMEM((2, cart), F32),
            pltpu.VMEM((1, hh), F32),
            pltpu.VMEM((4 * chans, ranges), BF),
            pltpu.VMEM((2, outs, ranges), BF),
            pltpu.VMEM((2, outs, ranges), BF),
            pltpu.VMEM((2, outs, ranges), BF),
            pltpu.VMEM((2, outs, ranges), BF),
            pltpu.VMEM((2, outs, ranges), F32),
            pltpu.VMEM((n * HALF, 4 * ranges), BF),
            pltpu.VMEM((n * HALF, 4 * ranges), BF),
            pltpu.VMEM((cart, n * HALF), BF),
            pltpu.VMEM((cart, n * HALF), BF),
            pltpu.VMEM((cart, 128), jnp.int32),
            pltpu.VMEM((cart, 128), F32),
            pltpu.VMEM((128, n), jnp.int32),
            pltpu.VMEM((groups, 2 * HALF, members), jnp.int32),
            pltpu.VMEM((groups, rows, 128), BF),
            pltpu.VMEM((groups, rows, 128), BF),
            pltpu.VMEM((2, 4 * ranges, 128), BF),
            pltpu.VMEM((n, 1, 128), jnp.int32),
            pltpu.VMEM((4, outs, hh), BF),
            pltpu.VMEM((2, hh, 512), BF),
            pltpu.VMEM((4, cart // 2, 128), BF),
            dma((10,)),
            dma((2,)),
            dma((2,)),
            dma((2,)),
            dma((2,)),
            dma,
            dma,
            dma((3,)),
            dma((3,)),
            dma((3,)),
            dma((3,)),
            dma((4, 3)),
            dma((4, 3)),
            dma((2, 3)),
            dma((2, 3)),
            dma((groups,)),
            dma((groups,)),
        ],
        compiler_params=pltpu.CompilerParams(
            collective_id=0, has_side_effects=True, vmem_limit_bytes=48 * 1024 * 1024
        ),
        cost_estimate=pl.CostEstimate(
            flops=4 * 10**9, bytes_accessed=2 * 10**6, transcendentals=0
        ),
    )(*[pltpu.with_memory_space_constraint(x, pltpu.HBM) for x in args])


def solution(mesh):
    return jax.shard_map(
        local,
        mesh=mesh,
        in_specs=(
            P(None, "az", None),
            P("ch", None, None, None),
            P("ch"),
            P("ch", None, None, None),
            P("ch"),
            P("az"),
            P(None, "az"),
            P(None, "az"),
            P("ch", None),
            P("ch"),
        ),
        out_specs=P("ch", "az"),
        check_vma=False,
    )
```
